128 devices in a mesh: row: 16 (over y, x), col: 8 (over z, core).
Axes of the slice: x: 4, y: 4, z: 4, core: 2. Of those that a mesh axis runs over, the one named last changes fastest.
Arguments:
- upper_block: float32 [2, 1024, 1024], P(None, 'row', 'col'), may hold values from -0.25 to 0.25
- block_inverse: float32 [2, 1024, 64], P(None, 'row'), may hold values from -0.375 to 0.375
- panel_rhs: float32 [2, 32, 1024], P(None, None, 'row'), may hold values from -6 to 6
- upper_trail: float32 [2, 1024, 131072], P(None, 'row', 'col'), may hold values from -0.125 to 0.125
- trail_rhs: float32 [2, 32, 131072], P(None, None, ('col', 'row')), may hold values from -6 to 6
- currents: float32 [2, 1024], P(None, 'row'), may hold values from -4 to 4
- owner: int32 [1024], P('row'), may hold values from 0 to 511
Outputs:
- panel_adjoint: float32 [2, 32, 1024], P(None, None, 'row')
- trail_updated: float32 [2, 32, 131072], P(None, None, ('col', 'row'))
- patch_gradient: float32 [512], P(('row', 'col'))
The draws below stay inside these ranges and needn't reach their ends.
Inputs may be any that keep to these rules, and one draw needn't show every extreme that they name: owner names a surface patch for each panel unknown.
All inputs are finite; a program needn't handle non-finite values.
Results may differ from the reference program's by a relative error of at most 0.0003.
Values sent between devices are 32-bit elements; how exact they have to be, the bound alone decides.
A program may use at most 64 MiB of HBM per device.

```python
import jax
import jax.numpy as jnp
from jax import lax

PANEL = 1024
NRHS = 32
PB = 64
TRAIL = 131072
PATCHES = 512


def touch_ends(entries, key, smallest, top_value):
    dims = entries.shape
    place = [jax.random.randint(jax.random.fold_in(key, axis), (), 0, dims[axis]) for axis in range(len(dims))]
    entries = entries.at[tuple(place)].set(smallest)
    longest = dims.index(max(dims))
    place[longest] = (place[longest] + 1) % dims[longest]
    return entries.at[tuple(place)].set(top_value)


def shard_levels(own_key, extent, shards, smallest, top_value):
    def one(axis_at, shards_of):
        draws = jax.random.uniform(jax.random.fold_in(jax.random.fold_in(own_key, 6), axis_at), (shards_of,), jnp.float32, smallest / len(shards), top_value / len(shards))
        return jnp.repeat(jnp.exp(draws), extent[axis_at] // shards_of).reshape((-1,) + (1,) * (len(extent) - axis_at - 1))

    level = one(*shards[0])
    for cut in shards[1:]:
        level = level * one(*cut)
    return level


def noise(stream_key, dims, deviation, bound, pieces=(), dtype=jnp.bfloat16):
    entries = jax.random.normal(stream_key, dims, jnp.float32) * deviation
    if len(pieces) > 0:
        entries = shard_levels(stream_key, dims, pieces, -0.22, 0.18) * entries
    return jnp.clip(entries, min=-bound, max=bound).astype(dtype)


def setup_inputs(seed: int = 0) -> dict:
    keys = jax.random.split(jax.random.key(seed), 8)
    return {
        "upper_block": noise(keys[0], (2, PANEL, PANEL), (8 * PB) ** -0.5, 0.25, ((1, 16), (2, 8)), jnp.float32),
        "block_inverse": noise(keys[1], (2, PANEL, PB), (4 * PB) ** -0.5, 0.375, ((1, 16),), jnp.float32),
        "panel_rhs": noise(keys[2], (2, NRHS, PANEL), 1.0, 6.0, ((2, 16),), jnp.float32),
        "upper_trail": noise(keys[3], (2, PANEL, TRAIL), (2 * PANEL) ** -0.5, 0.125, ((1, 16), (2, 8)), jnp.float32),
        "trail_rhs": noise(keys[4], (2, NRHS, TRAIL), 1.0, 6.0, ((2, 128),), jnp.float32),
        "currents": noise(keys[5], (2, PANEL), 0.3, 4.0, ((1, 16),), jnp.float32),
        "owner": touch_ends(jax.random.randint(keys[6], (PANEL,), 0, PATCHES), jax.random.fold_in(keys[6], 1), 0, PATCHES - 1).astype(jnp.int32),
    }


highest = lax.Precision.HIGHEST


def product_high(first, second):
    return jnp.dot(first, second, precision=highest, preferred_element_type=jnp.float32)


def conj_product(left, right):
    real_part = product_high(left[0], right[0]) + product_high(left[1], right[1])
    imag_part = product_high(left[1], right[0]) - product_high(left[0], right[1])
    return jnp.stack([real_part, imag_part])


def sweep(upper, inverses, rhs, width):
    count = rhs.shape[2] // width
    held_start = jnp.zeros(rhs.shape, jnp.float32)
    solved_start = jnp.zeros(rhs.shape, jnp.float32)

    def advance(index, carry):
        held, solved = carry
        start = (jnp.asarray(index) * width).astype(jnp.int32)
        local = lax.dynamic_slice_in_dim(held, start, width, 2)
        residual = lax.dynamic_slice_in_dim(rhs, start, width, 2) - local
        inverse = lax.dynamic_slice_in_dim(inverses, start, width, 1)
        value = conj_product(residual, inverse)
        rows_here = lax.dynamic_slice_in_dim(upper, start, width, 1)
        held = held + conj_product(value, rows_here)
        solved = lax.dynamic_update_slice_in_dim(solved, value, start, 2)
        return held, solved

    return lax.fori_loop(0, count, advance, (held_start, solved_start))[1]


def reference(upper_block, block_inverse, panel_rhs, upper_trail, trail_rhs, currents, owner):
    solved = sweep(upper_block, block_inverse, panel_rhs, PB)
    updated = trail_rhs - conj_product(solved, upper_trail)
    total = jnp.sum(solved, axis=1)
    partial_value = currents[0] * total[0] - currents[1] * total[1]
    gradient = jax.ops.segment_sum(partial_value, owner, num_segments=PATCHES)
    return solved, updated, gradient
```

```python
import jax
import jax.numpy as jnp
from jax import lax
from jax.experimental import pallas as pl
from jax.experimental.pallas import tpu as pltpu
from jax.sharding import PartitionSpec as P

MESH = pl.DeviceIdType.MESH
F32 = jnp.float32
BF16 = jnp.bfloat16
Y, X, Z = 0, 1, 2
DISTS = (1, 3, 2)
ORDER = (2, 1, 3, 0)


def halves(value):
    high = value.astype(BF16)
    low = (value - high.astype(F32)).astype(BF16)
    return high, low


def stacked(value):
    high, low = halves(value)
    return jnp.concatenate([high, low], axis=0)


def left_side(value):
    high, low = halves(value)
    both = jnp.concatenate([high, low], axis=0)
    return jnp.concatenate([both, both], axis=1)


def multiply(left, right):
    out = jnp.dot(left, right, preferred_element_type=F32)
    rows = out.shape[0] // 2
    return out[:rows] + out[rows:]


def conj_left(value):
    re, im = value[:, :64], value[:, 64:]
    turned = jnp.concatenate([im, -re], axis=1)
    return left_side(jnp.concatenate([value, turned], axis=0))


class Message:
    def __init__(self, where, cond, dim, dist, send, recv):
        self.where, self.cond, self.dim, self.dist = where, cond, dim, dist
        self.send, self.recv = send, recv


def body(
    upper_ref, inverse_ref, rhs_ref, trail_hbm, trail_rhs_hbm, currents_ref, owner_ref,
    solved_ref, updated_ref, gradient_ref,
    pieces, rhs_all, held, answers, trail, trail_rhs,
    first_out, first_in, second_out, second_in, third_out, third_in, fourth_in, tiles,
    local_sem, g_send, g_recv, k_send, k_recv, r_send, r_recv, t_send, t_recv,
):
    row, col = lax.axis_index("row"), lax.axis_index("col")
    me = (row // 4, row % 4, col // 2)
    core = col % 2

    def shifted(coords, dim, dist):
        moved = list(coords)
        moved[dim] = (moved[dim] + dist) % 4
        return tuple(moved)

    def device(coords, which):
        return (coords[0] * 4 + coords[1], coords[2] * 2 + which)

    def peer(dim, dist):
        if dim is None:
            return device(me, 1 - core)
        return device(shifted(me, dim, dist), core)

    loads = []
    for part in range(4):
        cols = pl.ds(part * 4096, 4096)
        loads.append(pltpu.make_async_copy(trail_hbm.at[:, :, cols], trail.at[:, :, cols], local_sem.at[part]))
    loads.append(pltpu.make_async_copy(trail_rhs_hbm, trail_rhs, local_sem.at[4]))
    for load in loads:
        load.start()

    barrier = pltpu.get_barrier_semaphore()
    for dim in (Y, X, Z):
        for dist in DISTS:
            pl.semaphore_signal(barrier, inc=1, device_id=peer(dim, dist), device_id_type=MESH)
    pl.semaphore_signal(barrier, inc=1, device_id=peer(None, 0), device_id_type=MESH)

    upper = upper_ref[...].reshape(128, 128)
    inv_re, inv_im = inverse_ref[0], inverse_ref[1]
    left = jnp.concatenate(
        [jnp.concatenate([inv_re, -inv_im], axis=1), jnp.concatenate([inv_im, inv_re], axis=1)], axis=0
    )
    pieces[me[0], me[1], me[2], core] = multiply(left_side(left), stacked(upper))
    rhs_all[me[0], me[1]] = jnp.concatenate([rhs_ref[0], rhs_ref[1]], axis=1)

    pl.semaphore_wait(barrier, 10)

    def copy_of(message, coords):
        ref = message.where(coords)
        return pltpu.make_async_remote_copy(
            src_ref=ref, dst_ref=ref, send_sem=message.send, recv_sem=message.recv,
            device_id=peer(message.dim, message.dist), device_id_type=MESH,
        )

    def guarded(cond, action):
        if cond is True:
            action()
        else:
            pl.when(cond)(action)

    def start(message):
        guarded(message.cond(me), lambda: copy_of(message, me).start())

    def source(message):
        return me if message.dim is None else shifted(me, message.dim, -message.dist + 4)

    def arrived(message):
        coords = source(message)
        guarded(message.cond(coords), lambda: copy_of(message, coords).wait_recv())

    def sent(message):
        guarded(message.cond(me), lambda: copy_of(message, me).wait_send())

    count = [0]
    forwards = []

    def message(where, cond, dim, dist):
        slot = count[0]
        count[0] += 1
        return Message(where, cond, dim, dist, g_send.at[slot], g_recv.at[slot])

    def forward(received):
        slot = len(forwards)
        coords = source(received)
        cond = received.cond(coords)

        def make(which):
            ref = received.where(coords, which)
            return pltpu.make_async_remote_copy(
                src_ref=ref, dst_ref=ref, send_sem=k_send.at[slot], recv_sem=k_recv.at[slot],
                device_id=peer(None, 0), device_id_type=MESH,
            )

        guarded(cond, lambda: make(core).start())
        forwards.append((cond, make))

    always = lambda c: True
    upper_half = lambda c: c[0] <= c[2]

    def stage_messages(rows, dims, groups):
        out = []
        for dim, group in zip(dims, groups):
            stage = []
            for dist in DISTS:
                for where, cond in group:
                    stage.append(message(where, cond, dim, dist))
            out.append(stage)
        return out

    def own(rows):
        return [(lambda c, k=core: pieces.at[c[0], c[1], c[2], k, rows], upper_half)]

    rows_a, rows_b, rows_c = pl.ds(0, 64), pl.ds(64, 32), pl.ds(96, 32)
    part_a = stage_messages(rows_a, (Z, Y, X), [
        own(rows_a),
        [(lambda c, k=core, z=z: pieces.at[c[0], c[1], z, k, rows_a], lambda c, z=z: c[0] <= z) for z in range(4)],
        [(lambda c, k=core, y=y: pieces.at[y, c[1], pl.ds(y, 4 - y), k, rows_a], always) for y in range(4)],
    ])
    part_b = stage_messages(rows_b, (X, Z, Y), [
        own(rows_b),
        [(lambda c, k=core: pieces.at[c[0], :, c[2], k, rows_b], upper_half)],
        [(lambda c, k=core, z=z: pieces.at[c[0], :, z, k, rows_b], lambda c, z=z: c[0] <= z) for z in range(4)],
    ])
    part_c = stage_messages(rows_c, (Y, X, Z), [
        own(rows_c),
        [(lambda c, k=core, y=y: pieces.at[y, c[1], c[2], k, rows_c], lambda c, y=y: y <= c[2]) for y in range(4)],
        [(lambda c, k=core, y=y: pieces.at[y, :, c[2], k, rows_c], lambda c, y=y: y <= c[2]) for y in range(4)],
    ])

    def half_rhs(c, k=core):
        return rhs_all.at[c[0], c[1], pl.ds(pl.multiple_of(k * 16, 16), 16)]

    def half_rhs_row(c, k=core):
        return rhs_all.at[c[0], :, pl.ds(pl.multiple_of(k * 16, 16), 16)]

    part_r = stage_messages(None, (X, Y), [[(half_rhs, always)], [(half_rhs_row, always)]])

    mine = Message(lambda c, k=core: pieces.at[c[0], c[1], c[2], k], upper_half, None, 0, None, None)
    stages = [
        part_r[0] + part_a[0] + part_b[0] + part_c[0],
        part_r[1] + part_a[1] + part_b[1] + part_c[1],
        part_a[2] + part_b[2] + part_c[2],
    ]
    for number, stage in enumerate(stages):
        for item in stage:
            start(item)
        if number == 0:
            forward(mine)
        interleaved = sorted(range(len(stage)), key=lambda i: DISTS.index(stage[i].dist))
        for i in interleaved:
            arrived(stage[i])
            forward(stage[i])
    for cond, make in forwards:
        guarded(cond, lambda make=make: make(1 - core).wait_recv())

    held[...] = jnp.zeros_like(held)
    lanes = lax.broadcasted_iota(jnp.int32, (32, 128), 1)
    for k in range(16):
        tile = held[:, (k // 2) * 128:(k // 2 + 1) * 128]
        if k % 2 == 0:
            local = jnp.where(lanes < 64, tile[:32], pltpu.roll(tile[32:], 64, 1))
        else:
            local = jnp.where(lanes < 64, pltpu.roll(tile[:32], 64, 1), tile[32:])
        value = rhs_all[k // 4, k % 4] - local
        answers[k] = value
        first = (k + 1) // 2
        if first < 8:
            lhs = conj_left(value)
            for c in range(first, 8):
                rhs = stacked(pieces[k // 4, k % 4, c // 2, c % 2])
                held[:, c * 128:(c + 1) * 128] += multiply(lhs, rhs)

    value = multiply(conj_left(answers[row]), stacked(inverse_ref[...].reshape(128, 64)))
    solved_ref[...] = value.reshape(2, 32, 64)
    lhs = conj_left(jnp.concatenate([value[:32], value[32:]], axis=1))

    total_re = jnp.sum(value[:32], axis=0, keepdims=True)
    total_im = jnp.sum(value[32:], axis=0, keepdims=True)
    partial_value = currents_ref[0:1, :] * total_re - currents_ref[1:2, :] * total_im
    tiles[me[0], me[1], 0:1, 0:64] = partial_value
    tiles[me[0], me[1], 1:2, 0:64] = owner_ref[...].astype(F32)
    tiles[me[0], me[1], 0:2, 64:128] = jnp.full((2, 64), -1.0, F32)
    tiles[me[0], me[1], 2:8, :] = jnp.zeros((6, 128), F32)
    tile_messages = []
    for n, (dim, where) in enumerate(((X, lambda c: tiles.at[c[0], c[1]]), (Y, lambda c: tiles.at[c[0]]))):
        tile_messages.append([Message(where, always, dim, d, t_send.at[n, i], t_recv.at[n, i]) for i, d in enumerate(DISTS)])
    for item in tile_messages[0]:
        start(item)

    for load in loads:
        load.wait()

    def term(half, a, j):
        dims = (X, Y) if half == 0 else (Y, X)
        there = shifted(shifted(me, dims[0], a), dims[1], j)
        begin = pl.multiple_of((there[0] * 4 + there[1]) * 1024 + half * 512, 512)
        block = trail[:, :, pl.ds(begin, 512)].reshape(128, 512)
        return multiply(lhs, stacked(block))

    def send(src, dst, dim, dist, slot):
        copy = pltpu.make_async_remote_copy(
            src_ref=src, dst_ref=dst, send_sem=r_send.at[slot], recv_sem=r_recv.at[slot],
            device_id=peer(dim, dist), device_id_type=MESH,
        )
        copy.start()
        return copy

    DIM = ((X, Y), (Y, X))
    top, low = pl.ds(0, 32), pl.ds(32, 32)
    one, two, three, four = {}, {}, {}, {}
    for n, j in enumerate(ORDER):
        for h in range(2):
            first_out[h, n] = term(h, 2, j)
            slot = (h * 4 + n) * 2
            one[h, n, 0] = send(first_out.at[h, n, top], first_in.at[h, n, 0], DIM[h][0], 1, slot)
            one[h, n, 1] = send(first_out.at[h, n, low], first_in.at[h, n, 1], DIM[h][0], 3, slot + 1)
        if n == 0:
            for item in tile_messages[0]:
                arrived(item)
            for item in tile_messages[1]:
                start(item)
    for n, j in enumerate(ORDER):
        for h in range(2):
            slot = 16 + (h * 4 + n) * 2
            for s, a in enumerate((1, 3)):
                second_out[h, n, s] = term(h, a, j)
                one[h, n, s].wait_recv()
                rows = top if s == 0 else low
                second_out[h, n, s, rows] += first_in[h, n, s]
                two[h, n, s] = send(second_out.at[h, n, s], second_in.at[h, n, s], DIM[h][0], a, slot + s)
    for n, j in enumerate(ORDER):
        for h in range(2):
            third_out[h, n] = term(h, 0, j)
            for s in range(2):
                two[h, n, s].wait_recv()
            third_out[h, n] += second_in[h, n, 0] + second_in[h, n, 1]
            if j == 2:
                three[h, 0] = send(third_out.at[h, n, top], third_in.at[h, 0], DIM[h][1], 1, 32 + h * 4)
                three[h, 1] = send(third_out.at[h, n, low], third_in.at[h, 1], DIM[h][1], 3, 33 + h * 4)
            elif j == 0:
                for s in range(2):
                    four[h, s].wait_recv()
                total = third_out[h, n] + fourth_in[h, 0] + fourth_in[h, 1]
                cols = pl.ds(h * 512, 512)
                updated_ref[:, :, cols] = trail_rhs[:, :, cols] - total.reshape(2, 32, 512)
            else:
                s = 0 if j == 1 else 1
                rows = top if s == 0 else low
                three[h, s].wait_recv()
                third_out[h, n, rows] += third_in[h, s]
                four[h, s] = send(third_out.at[h, n], fourth_in.at[h, s], DIM[h][1], j, 34 + h * 4 + s)

    for item in tile_messages[1]:
        arrived(item)
    parts = tiles[...].reshape(16, 8, 128)
    for n in range(4):
        patch = ((row * 8 + col) * 4 + n).astype(F32)
        chosen = jnp.where(parts[:, 1, :] == patch, parts[:, 0, :], 0.0)
        gradient_ref[n] = jnp.sum(chosen)

    for stage in stages:
        for item in stage:
            sent(item)
    for cond, make in forwards:
        guarded(cond, lambda make=make: make(core).wait_send())
    for group in tile_messages:
        for item in group:
            sent(item)
    for group in (one, two, three, four):
        for copy in group.values():
            copy.wait_send()


def on_device(upper_block, block_inverse, panel_rhs, upper_trail, trail_rhs, currents, owner):
    vmem = pl.BlockSpec(memory_space=pltpu.VMEM)
    anywhere = pl.BlockSpec(memory_space=pl.ANY)
    dma = pltpu.SemaphoreType.DMA
    return pl.pallas_call(
        body,
        out_shape=(
            jax.ShapeDtypeStruct((2, 32, 64), F32),
            jax.ShapeDtypeStruct((2, 32, 1024), F32),
            jax.ShapeDtypeStruct((4,), F32),
        ),
        in_specs=[vmem, vmem, vmem, anywhere, anywhere, vmem, vmem],
        out_specs=(vmem, vmem, pl.BlockSpec(memory_space=pltpu.SMEM)),
        scratch_shapes=[
            pltpu.VMEM((4, 4, 4, 2, 128, 128), F32),
            pltpu.VMEM((4, 4, 32, 128), F32),
            pltpu.VMEM((64, 1024), F32),
            pltpu.VMEM((16, 32, 128), F32),
            pltpu.VMEM((2, 64, 16384), F32),
            pltpu.VMEM((2, 32, 1024), F32),
            pltpu.VMEM((2, 4, 64, 512), F32),
            pltpu.VMEM((2, 4, 2, 32, 512), F32),
            pltpu.VMEM((2, 4, 2, 64, 512), F32),
            pltpu.VMEM((2, 4, 2, 64, 512), F32),
            pltpu.VMEM((2, 4, 64, 512), F32),
            pltpu.VMEM((2, 2, 32, 512), F32),
            pltpu.VMEM((2, 2, 64, 512), F32),
            pltpu.VMEM((4, 4, 8, 128), F32),
            dma((5,)),
            dma((80,)), dma((80,)),
            dma((80,)), dma((80,)),
            dma((40,)), dma((40,)),
            dma((2, 3)), dma((2, 3)),
        ],
        compiler_params=pltpu.CompilerParams(
            collective_id=0, has_side_effects=True, vmem_limit_bytes=48 * 2**20
        ),
        name="panel",
    )(upper_block, block_inverse, panel_rhs, upper_trail, trail_rhs, currents, owner.reshape(1, 64))


def solution(mesh):
    return jax.shard_map(
        on_device,
        mesh=mesh,
        in_specs=(
            P(None, "row", "col"),
            P(None, "row", None),
            P(None, None, "row"),
            P(None, "row", "col"),
            P(None, None, ("col", "row")),
            P(None, "row"),
            P("row"),
        ),
        out_specs=(P(None, None, "row"), P(None, None, ("col", "row")), P(("row", "col"))),
        check_vma=False,
    )
```

```python
import jax
import jax.numpy as jnp
from jax import lax
from jax.experimental import pallas as pl
from jax.experimental.pallas import tpu as pltpu
from jax.sharding import PartitionSpec as P

MESH = pl.DeviceIdType.MESH
F32 = jnp.float32
BF16 = jnp.bfloat16
Y, X, Z = 0, 1, 2
DISTS = (1, 3, 2)
ORDER = (2, 1, 3, 0)


def halves(value):
    high = value.astype(BF16)
    low = (value - high.astype(F32)).astype(BF16)
    return high, low


def stacked(value):
    high, low = halves(value)
    return jnp.concatenate([high, low], axis=0)


def left_side(value):
    high, low = halves(value)
    both = jnp.concatenate([high, low], axis=0)
    return jnp.concatenate([both, both], axis=1)


def multiply(left, right):
    out = jnp.dot(left, right, preferred_element_type=F32)
    rows = out.shape[0] // 2
    return out[:rows] + out[rows:]


def conj_left(value):
    re, im = value[:, :64], value[:, 64:]
    turned = jnp.concatenate([im, -re], axis=1)
    return left_side(jnp.concatenate([value, turned], axis=0))


def body(
    upper_hbm, inverse_hbm, rhs_hbm, trail_hbm, trail_rhs_hbm, currents_hbm, owner_hbm,
    solved_ref, updated_ref, gradient_ref,
    upper_ref, inverse_ref, rhs_ref, currents_ref, owner_ref, pieces, rhs_all, held, answers, weights, trail, trail_rhs,
    first_out, first_in, second_out, second_in, third_out, third_in, fourth_in, tiles,
    local_sem, r_send, r_recv, *pairs,
):
    (y_sems, x_sems, z_sems, rhs_sems, k_sems, chain_sems, tile_sems) = zip(
        pairs[::2], pairs[1::2]
    )
    row, col = lax.axis_index("row"), lax.axis_index("col")
    me = (row // 4, row % 4, col // 2)
    core = col % 2

    def shifted(coords, dim, dist):
        moved = list(coords)
        moved[dim] = (moved[dim] + dist) % 4
        return tuple(moved)

    def device(coords, which):
        return (coords[0] * 4 + coords[1], coords[2] * 2 + which)

    def peer(dim, dist):
        if dim is None:
            return device(me, 1 - core)
        return device(shifted(me, dim, dist), core)

    early = []
    for n, (src, dst) in enumerate((
        (upper_hbm, upper_ref), (inverse_hbm, inverse_ref), (rhs_hbm, rhs_ref), (currents_hbm, currents_ref), (owner_hbm, owner_ref)
    )):
        early.append(pltpu.make_async_copy(src, dst, local_sem.at[5 + n]))
        early[n].start()
    loads = []
    for part in range(4):
        cols = pl.ds(part * 4096, 4096)
        loads.append(pltpu.make_async_copy(trail_hbm.at[:, :, cols], trail.at[:, :, cols], local_sem.at[part]))
    loads.append(pltpu.make_async_copy(trail_rhs_hbm, trail_rhs, local_sem.at[4]))
    for load in loads:
        load.start()

    barrier = pltpu.get_barrier_semaphore()
    for dim in (Y, X, Z):
        for dist in DISTS:
            pl.semaphore_signal(barrier, inc=1, device_id=peer(dim, dist), device_id_type=MESH)
    pl.semaphore_signal(barrier, inc=1, device_id=peer(None, 0), device_id_type=MESH)
    for dist in DISTS:
        there = shifted(shifted(me, Y, dist), Z, dist)
        pl.semaphore_signal(barrier, inc=1, device_id=device(there, core), device_id_type=MESH)

    for load in early:
        load.wait()

    upper = upper_ref[...].reshape(128, 128)
    inv_re, inv_im = inverse_ref[0], inverse_ref[1]
    left = jnp.concatenate(
        [jnp.concatenate([inv_re, -inv_im], axis=1), jnp.concatenate([inv_im, inv_re], axis=1)], axis=0
    )
    pieces[me[0], me[1], core] = multiply(left_side(left), stacked(upper))
    rhs_all[me[1]] = jnp.concatenate([rhs_ref[0], rhs_ref[1]], axis=1)

    pl.semaphore_wait(barrier, 13)

    y, x, z = me

    def turn(at, dist):
        moved = at + dist
        return jnp.where(moved >= 4, moved - 4, moved)

    FULL = (0,) + DISTS
    from_y = [turn(y, (4 - d) % 4) for d in FULL]
    from_x = [turn(x, (4 - d) % 4) for d in FULL]
    to_y = [turn(y, d) for d in FULL]
    to_x = [turn(x, d) for d in FULL]
    to_z = [turn(z, d) for d in FULL]
    peers = {
        Y: [(v * 4 + x, col) for v in to_y],
        X: [(y * 4 + v, col) for v in to_x],
        Z: [(row, v * 2 + core) for v in to_z],
        None: [(row, col + 1 - 2 * core)] * 4,
        "YZ": [(v * 4 + x, w * 2 + core) for v, w in zip(to_y, to_z)],
    }
    solver = y == z
    three = range(3)

    def both(first, second):
        return jnp.logical_and(first, second)

    def remote(ref, dim, i, sems, index, there=None):
        return pltpu.make_async_remote_copy(
            src_ref=ref, dst_ref=ref, send_sem=sems[0].at[index], recv_sem=sems[1].at[index if there is None else there],
            device_id=peers[dim][i + 1], device_id_type=MESH,
        )

    def run(what, cond, ref, dim, i, sems, index, there=None):
        pl.when(cond)(lambda: getattr(remote(ref(), dim, i, sems, index, there), what)())

    def needed(py, px, which):
        return jnp.logical_or(py < y, both(py == y, (px + 1) // 2 <= which))

    def go_y(what, i):
        if what == "wait_recv":
            py, cond = from_y[i + 1], both(solver, from_y[i + 1] < y)
        else:
            py, cond = y, both(y < z, to_y[i + 1] == z)
        run(what, cond, lambda: pieces.at[py, x, core], Y, i, y_sems, i)

    def go_x(what, py, i):
        px = from_x[i + 1] if what == "wait_recv" else x
        run(what, both(both(solver, py <= y), needed(py, px, core)), lambda: pieces.at[py, px, core], X, i, x_sems, (py, i))

    def go_r(what, i):
        px = from_x[i + 1] if what == "wait_recv" else x
        run(what, solver, lambda: rhs_all.at[px], X, i, rhs_sems, i)

    def go_k(what, py, px):
        which = 1 - core if what == "wait_recv" else core
        run(what, both(both(solver, py <= y), needed(py, px, which)), lambda: pieces.at[py, px, which], None, 0, k_sems, (py, px))

    def go_chain(what, i):
        if what == "wait_recv":
            at, cond = from_y[i + 1], both(solver, from_y[i + 1] < y)
        else:
            at, cond = y, both(solver, y < to_y[i + 1])
        run(what, cond, lambda: answers.at[at], "YZ", i, chain_sems, i, i)

    def go_z(what, i):
        cond = turn(z, 4 - DISTS[i]) == y if what == "wait_recv" else solver
        run(what, cond, lambda: answers.at[y, x], Z, i, z_sems, i)

    for i in three:
        go_y("start", i)
    for i in three:
        go_r("start", i)
        go_x("start", y, i)
    go_k("start", y, x)
    for i in three:
        go_y("wait_recv", i)
        for j in three:
            pl.when(from_y[i + 1] < y)(lambda i=i, j=j: go_x("start", from_y[i + 1], j))
        pl.when(from_y[i + 1] < y)(lambda i=i: go_k("start", from_y[i + 1], x))

    def upto(count, action):
        def step(index, carry):
            action(index)
            return carry
        lax.fori_loop(0, count, step, 0)

    lanes = lax.broadcasted_iota(jnp.int32, (32, 128), 1)

    @pl.when(solver)
    def _():
        def collect(py):
            for i in three:
                go_x("wait_recv", py, i)
                go_k("start", py, from_x[i + 1])

        upto(y + 1, collect)
        for i in three:
            go_r("wait_recv", i)

        def split(py):
            for px in range(4):
                go_k("wait_recv", py, px)
            for px in range(4):
                for which in range(2):
                    weights[py, px, :, which * 128:(which + 1) * 128] = stacked(pieces[py, px, which])

        upto(y + 1, split)
        held[...] = jnp.zeros_like(held)

        def earlier(at):
            for i in three:
                pl.when(from_y[i + 1] == at)(lambda i=i: go_chain("wait_recv", i))
            total = held[...]
            for px in range(4):
                total = total + multiply(conj_left(answers[at, px]), weights[at, px])
            held[...] = total

        upto(y, earlier)
        for n in range(4):
            tile = held[:, (n // 2) * 128:(n // 2 + 1) * 128]
            if n % 2 == 0:
                local = jnp.where(lanes < 64, tile[:32], pltpu.roll(tile[32:], 64, 1))
            else:
                local = jnp.where(lanes < 64, pltpu.roll(tile[:32], 64, 1), tile[32:])
            answer = rhs_all[n] - local
            answers[y, n] = answer
            first = (n + 1) // 2 * 128
            if first < 256:
                held[:, first:] += multiply(conj_left(answer), weights[y, n, :, first:])

    for i in three:
        go_chain("start", i)
    for i in three:
        go_z("start", i)
    for i in three:
        go_z("wait_recv", i)

    value = multiply(conj_left(answers[y, x]), stacked(inverse_ref[...].reshape(128, 64)))
    solved_ref[...] = value.reshape(2, 32, 64)
    lhs = conj_left(jnp.concatenate([value[:32], value[32:]], axis=1))

    total_re = jnp.sum(value[:32], axis=0, keepdims=True)
    total_im = jnp.sum(value[32:], axis=0, keepdims=True)
    partial_value = currents_ref[0:1, :] * total_re - currents_ref[1:2, :] * total_im
    tiles[me[0], me[1], 0:1, 0:64] = partial_value
    tiles[me[0], me[1], 1:2, 0:64] = owner_ref[...].astype(F32)
    tiles[me[0], me[1], 0:2, 64:128] = jnp.full((2, 64), -1.0, F32)
    tiles[me[0], me[1], 2:8, :] = jnp.zeros((6, 128), F32)
    def go_t(what, n, i):
        recv = what == "wait_recv"
        if n == 0:
            ref = tiles.at[y, from_x[i + 1] if recv else x]
        else:
            ref = tiles.at[from_y[i + 1] if recv else y]
        getattr(remote(ref, X if n == 0 else Y, i, tile_sems, (n, i)), what)()

    for i in three:
        go_t("start", 0, i)

    for load in loads:
        load.wait()

    def term(half, a, j):
        dims = (X, Y) if half == 0 else (Y, X)
        there = shifted(shifted(me, dims[0], a), dims[1], j)
        begin = pl.multiple_of((there[0] * 4 + there[1]) * 1024 + half * 512, 512)
        block = trail[:, :, pl.ds(begin, 512)].reshape(128, 512)
        return multiply(lhs, stacked(block))

    def send(src, dst, dim, dist, slot):
        copy = pltpu.make_async_remote_copy(
            src_ref=src, dst_ref=dst, send_sem=r_send.at[slot], recv_sem=r_recv.at[slot],
            device_id=peer(dim, dist), device_id_type=MESH,
        )
        copy.start()
        return copy

    DIM = ((X, Y), (Y, X))
    top, low = pl.ds(0, 32), pl.ds(32, 32)
    one, two, third, fourth = {}, {}, {}, {}
    for n, j in enumerate(ORDER):
        for h in range(2):
            first_out[h, n] = term(h, 2, j)
            slot = (h * 4 + n) * 2
            one[h, n, 0] = send(first_out.at[h, n, top], first_in.at[h, n, 0], DIM[h][0], 1, slot)
            one[h, n, 1] = send(first_out.at[h, n, low], first_in.at[h, n, 1], DIM[h][0], 3, slot + 1)
        if n == 0:
            for i in three:
                go_t("wait_recv", 0, i)
            for i in three:
                go_t("start", 1, i)
    for n, j in enumerate(ORDER):
        for h in range(2):
            slot = 16 + (h * 4 + n) * 2
            for s, a in enumerate((1, 3)):
                second_out[h, n, s] = term(h, a, j)
                one[h, n, s].wait_recv()
                rows = top if s == 0 else low
                second_out[h, n, s, rows] += first_in[h, n, s]
                two[h, n, s] = send(second_out.at[h, n, s], second_in.at[h, n, s], DIM[h][0], a, slot + s)
    for n, j in enumerate(ORDER):
        for h in range(2):
            third_out[h, n] = term(h, 0, j)
            for s in range(2):
                two[h, n, s].wait_recv()
            third_out[h, n] += second_in[h, n, 0] + second_in[h, n, 1]
            if j == 2:
                third[h, 0] = send(third_out.at[h, n, top], third_in.at[h, 0], DIM[h][1], 1, 32 + h * 4)
                third[h, 1] = send(third_out.at[h, n, low], third_in.at[h, 1], DIM[h][1], 3, 33 + h * 4)
            elif j == 0:
                for s in range(2):
                    fourth[h, s].wait_recv()
                total = third_out[h, n] + fourth_in[h, 0] + fourth_in[h, 1]
                cols = pl.ds(h * 512, 512)
                updated_ref[:, :, cols] = trail_rhs[:, :, cols] - total.reshape(2, 32, 512)
            else:
                s = 0 if j == 1 else 1
                rows = top if s == 0 else low
                third[h, s].wait_recv()
                third_out[h, n, rows] += third_in[h, s]
                fourth[h, s] = send(third_out.at[h, n], fourth_in.at[h, s], DIM[h][1], j, 34 + h * 4 + s)

    for i in three:
        go_t("wait_recv", 1, i)
    parts = tiles[...].reshape(16, 8, 128)
    for n in range(4):
        patch = ((row * 8 + col) * 4 + n).astype(F32)
        chosen = jnp.where(parts[:, 1, :] == patch, parts[:, 0, :], 0.0)
        gradient_ref[n] = jnp.sum(chosen)

    for i in three:
        go_y("wait_send", i)
        go_r("wait_send", i)
        go_chain("wait_send", i)
        go_z("wait_send", i)
        for n in range(2):
            go_t("wait_send", n, i)
    for py in range(4):
        for i in three:
            go_x("wait_send", py, i)
        for px in range(4):
            go_k("wait_send", py, px)
    for group in (one, two, third, fourth):
        for copy in group.values():
            copy.wait_send()


def on_device(upper_block, block_inverse, panel_rhs, upper_trail, trail_rhs, currents, owner):
    vmem = pl.BlockSpec(memory_space=pltpu.VMEM)
    hbm = pl.BlockSpec(memory_space=pltpu.HBM)
    dma = pltpu.SemaphoreType.DMA
    return pl.pallas_call(
        body,
        out_shape=(
            jax.ShapeDtypeStruct((2, 32, 64), F32),
            jax.ShapeDtypeStruct((2, 32, 1024), F32),
            jax.ShapeDtypeStruct((4,), F32),
        ),
        in_specs=[hbm] * 7,
        out_specs=(vmem, vmem, pl.BlockSpec(memory_space=pltpu.SMEM)),
        scratch_shapes=[
            pltpu.VMEM((2, 64, 128), F32),
            pltpu.VMEM((2, 64, 64), F32),
            pltpu.VMEM((2, 32, 64), F32),
            pltpu.VMEM((2, 64), F32),
            pltpu.VMEM((1, 64), jnp.int32),
            pltpu.VMEM((4, 4, 2, 128, 128), F32),
            pltpu.VMEM((4, 32, 128), F32),
            pltpu.VMEM((64, 256), F32),
            pltpu.VMEM((4, 4, 32, 128), F32),
            pltpu.VMEM((4, 4, 256, 256), BF16),
            pltpu.VMEM((2, 64, 16384), F32),
            pltpu.VMEM((2, 32, 1024), F32),
            pltpu.VMEM((2, 4, 64, 512), F32),
            pltpu.VMEM((2, 4, 2, 32, 512), F32),
            pltpu.VMEM((2, 4, 2, 64, 512), F32),
            pltpu.VMEM((2, 4, 2, 64, 512), F32),
            pltpu.VMEM((2, 4, 64, 512), F32),
            pltpu.VMEM((2, 2, 32, 512), F32),
            pltpu.VMEM((2, 2, 64, 512), F32),
            pltpu.VMEM((4, 4, 8, 128), F32),
            dma((10,)),
            dma((40,)), dma((40,)),
            *(
                dma(shape)
                for shape in (
                    (3,), (4, 3), (3,), (3,), (4, 4), (3,), (2, 3)
                )
                for _ in range(2)
            ),
        ],
        compiler_params=pltpu.CompilerParams(
            collective_id=0, has_side_effects=True, vmem_limit_bytes=63 * 2**20
        ),
        name="panel",
    )(upper_block, block_inverse, panel_rhs, upper_trail, trail_rhs, currents, owner.reshape(1, 64))


def solution(mesh):
    return jax.shard_map(
        on_device,
        mesh=mesh,
        in_specs=(
            P(None, "row", "col"),
            P(None, "row", None),
            P(None, None, "row"),
            P(None, "row", "col"),
            P(None, None, ("col", "row")),
            P(None, "row"),
            P("row"),
        ),
        out_specs=(P(None, None, "row"), P(None, None, ("col", "row")), P(("row", "col"))),
        check_vma=False,
    )
```

```python
import jax
import jax.numpy as jnp
from jax import lax
from jax.experimental import pallas as pl
from jax.experimental.pallas import tpu as pltpu
from jax.sharding import PartitionSpec as P

MESH = pl.DeviceIdType.MESH
F32 = jnp.float32
BF16 = jnp.bfloat16
Y, X, Z = 0, 1, 2
DISTS = (1, 3, 2)
ORDER = (2, 1, 3, 0)


def halves(value):
    high = value.astype(BF16)
    low = (value - high.astype(F32)).astype(BF16)
    return high, low


def stacked(value):
    high, low = halves(value)
    return jnp.concatenate([high, low], axis=0)


def left_side(value):
    high, low = halves(value)
    both = jnp.concatenate([high, low], axis=0)
    return jnp.concatenate([both, both], axis=1)


def multiply(left, right):
    out = jnp.dot(left, right, preferred_element_type=F32)
    rows = out.shape[0] // 2
    return out[:rows] + out[rows:]


def conj_left(value):
    re, im = value[:, :64], value[:, 64:]
    turned = jnp.concatenate([im, -re], axis=1)
    return left_side(jnp.concatenate([value, turned], axis=0))


def body(
    upper_hbm, inverse_hbm, rhs_hbm, trail_hbm, trail_rhs_hbm, currents_hbm, owner_hbm,
    solved_ref, updated_ref, gradient_ref,
    upper_ref, inverse_ref, rhs_ref, currents_ref, owner_ref, pieces, rhs_all, held, answers, weights, trail, trail_rhs,
    first_out, first_in, second_out, second_in, third_out, third_in, fourth_in, tiles,
    local_sem, r_send, r_recv, *pairs,
):
    (y_sems, x_sems, z_sems, rhs_sems, k_sems, chain_sems, tile_sems) = zip(
        pairs[::2], pairs[1::2]
    )
    row, col = lax.axis_index("row"), lax.axis_index("col")
    me = (row // 4, row % 4, col // 2)
    core = col % 2

    def shifted(coords, dim, dist):
        moved = list(coords)
        moved[dim] = (moved[dim] + dist) % 4
        return tuple(moved)

    def device(coords, which):
        return (coords[0] * 4 + coords[1], coords[2] * 2 + which)

    def peer(dim, dist):
        if dim is None:
            return device(me, 1 - core)
        return device(shifted(me, dim, dist), core)

    early = []
    for n, (src, dst) in enumerate((
        (upper_hbm, upper_ref), (inverse_hbm, inverse_ref), (rhs_hbm, rhs_ref), (currents_hbm, currents_ref), (owner_hbm, owner_ref)
    )):
        early.append(pltpu.make_async_copy(src, dst, local_sem.at[5 + n]))
        early[n].start()
    loads = []
    for part in range(4):
        cols = pl.ds(part * 4096, 4096)
        loads.append(pltpu.make_async_copy(trail_hbm.at[:, :, cols], trail.at[:, :, cols], local_sem.at[part]))
    loads.append(pltpu.make_async_copy(trail_rhs_hbm, trail_rhs, local_sem.at[4]))
    for load in loads:
        load.start()

    barrier = pltpu.get_barrier_semaphore()
    for dim in (Y, X, Z):
        for dist in DISTS:
            pl.semaphore_signal(barrier, inc=1, device_id=peer(dim, dist), device_id_type=MESH)
    pl.semaphore_signal(barrier, inc=1, device_id=peer(None, 0), device_id_type=MESH)
    for dist in DISTS:
        there = shifted(shifted(me, Y, dist), Z, dist)
        pl.semaphore_signal(barrier, inc=1, device_id=device(there, core), device_id_type=MESH)

    for load in early:
        load.wait()

    upper = upper_ref[...].reshape(128, 128)
    inv_re, inv_im = inverse_ref[0], inverse_ref[1]
    left = jnp.concatenate(
        [jnp.concatenate([inv_re, -inv_im], axis=1), jnp.concatenate([inv_im, inv_re], axis=1)], axis=0
    )
    pieces[me[0], me[1], core] = multiply(left_side(left), stacked(upper))
    rhs_all[me[1]] = jnp.concatenate([rhs_ref[0], rhs_ref[1]], axis=1)

    pl.semaphore_wait(barrier, 13)

    y, x, z = me

    def turn(at, dist):
        moved = at + dist
        return jnp.where(moved >= 4, moved - 4, moved)

    FULL = (0,) + DISTS
    from_y = [turn(y, (4 - d) % 4) for d in FULL]
    from_x = [turn(x, (4 - d) % 4) for d in FULL]
    to_y = [turn(y, d) for d in FULL]
    to_x = [turn(x, d) for d in FULL]
    to_z = [turn(z, d) for d in FULL]
    peers = {
        Y: [(v * 4 + x, col) for v in to_y],
        X: [(y * 4 + v, col) for v in to_x],
        Z: [(row, v * 2 + core) for v in to_z],
        None: [(row, col + 1 - 2 * core)] * 4,
        "YZ": [(v * 4 + x, w * 2 + core) for v, w in zip(to_y, to_z)],
    }
    solver = y == z
    three = range(3)

    def both(first, second):
        return jnp.logical_and(first, second)

    def remote(ref, dim, i, sems, index, there=None):
        return pltpu.make_async_remote_copy(
            src_ref=ref, dst_ref=ref, send_sem=sems[0].at[index], recv_sem=sems[1].at[index if there is None else there],
            device_id=peers[dim][i + 1], device_id_type=MESH,
        )

    def run(what, cond, ref, dim, i, sems, index, there=None):
        pl.when(cond)(lambda: getattr(remote(ref(), dim, i, sems, index, there), what)())

    def needed(py, px, which):
        return jnp.logical_or(py < y, both(py == y, (px + 1) // 2 <= which))

    def go_y(what, i):
        if what == "wait_recv":
            py, cond = from_y[i + 1], both(solver, from_y[i + 1] < y)
        else:
            py, cond = y, both(y < z, to_y[i + 1] == z)
        run(what, cond, lambda: pieces.at[py, x, core], Y, i, y_sems, i)

    def go_x(what, py, i):
        px = from_x[i + 1] if what == "wait_recv" else x
        run(what, both(both(solver, py <= y), needed(py, px, core)), lambda: pieces.at[py, px, core], X, i, x_sems, (py, i))

    def go_r(what, i):
        px = from_x[i + 1] if what == "wait_recv" else x
        run(what, solver, lambda: rhs_all.at[px], X, i, rhs_sems, i)

    def go_k(what, py, px):
        which = 1 - core if what == "wait_recv" else core
        run(what, both(both(solver, py <= y), needed(py, px, which)), lambda: pieces.at[py, px, which], None, 0, k_sems, (py, px))

    def go_chain(what, i, n):
        if what == "wait_recv":
            at, cond = from_y[i + 1], both(solver, from_y[i + 1] < y)
        else:
            at, cond = y, both(solver, y < to_y[i + 1])
        run(what, cond, lambda: answers.at[at, n], "YZ", i, chain_sems, (i, n))

    def go_z(what, i):
        cond = turn(z, 4 - DISTS[i]) == y if what == "wait_recv" else solver
        run(what, cond, lambda: answers.at[y, x], Z, i, z_sems, i)

    for i in three:
        go_y("start", i)
    for i in three:
        go_r("start", i)
        go_x("start", y, i)
    go_k("start", y, x)
    for i in three:
        go_y("wait_recv", i)
        for j in three:
            pl.when(from_y[i + 1] < y)(lambda i=i, j=j: go_x("start", from_y[i + 1], j))
        pl.when(from_y[i + 1] < y)(lambda i=i: go_k("start", from_y[i + 1], x))

    def upto(count, action):
        def step(index, carry):
            action(index)
            return carry
        lax.fori_loop(0, count, step, 0)

    lanes = lax.broadcasted_iota(jnp.int32, (32, 128), 1)

    @pl.when(solver)
    def _():
        def collect(py):
            for i in three:
                go_x("wait_recv", py, i)
                go_k("start", py, from_x[i + 1])

        upto(y + 1, collect)
        for i in three:
            go_r("wait_recv", i)

        def split(py):
            for px in range(4):
                go_k("wait_recv", py, px)
            for px in range(4):
                for which in range(2):
                    weights[py, px, :, which * 128:(which + 1) * 128] = stacked(pieces[py, px, which])

        upto(y + 1, split)
        held[...] = jnp.zeros_like(held)

        def earlier(at):
            for px in range(4):
                for i in three:
                    pl.when(from_y[i + 1] == at)(lambda i=i: go_chain("wait_recv", i, px))
                held[...] += multiply(conj_left(answers[at, px]), weights[at, px])

        upto(y, earlier)
        for n in range(4):
            tile = held[:, (n // 2) * 128:(n // 2 + 1) * 128]
            if n % 2 == 0:
                local = jnp.where(lanes < 64, tile[:32], pltpu.roll(tile[32:], 64, 1))
            else:
                local = jnp.where(lanes < 64, pltpu.roll(tile[:32], 64, 1), tile[32:])
            answer = rhs_all[n] - local
            answers[y, n] = answer
            for i in three:
                pl.when(y < to_y[i + 1])(lambda i=i: go_chain("start", i, n))

            @pl.when(x == n)
            def _():
                for i in three:
                    go_z("start", i)

            first = (n + 1) // 2 * 128
            if first < 256:
                held[:, first:] += multiply(conj_left(answer), weights[y, n, :, first:])

    for i in three:
        go_z("wait_recv", i)

    value = multiply(conj_left(answers[y, x]), stacked(inverse_ref[...].reshape(128, 64)))
    solved_ref[...] = value.reshape(2, 32, 64)
    lhs = conj_left(jnp.concatenate([value[:32], value[32:]], axis=1))

    total_re = jnp.sum(value[:32], axis=0, keepdims=True)
    total_im = jnp.sum(value[32:], axis=0, keepdims=True)
    partial_value = currents_ref[0:1, :] * total_re - currents_ref[1:2, :] * total_im
    tiles[me[0], me[1], 0:1, 0:64] = partial_value
    tiles[me[0], me[1], 1:2, 0:64] = owner_ref[...].astype(F32)
    tiles[me[0], me[1], 0:2, 64:128] = jnp.full((2, 64), -1.0, F32)
    tiles[me[0], me[1], 2:8, :] = jnp.zeros((6, 128), F32)
    def go_t(what, n, i):
        recv = what == "wait_recv"
        if n == 0:
            ref = tiles.at[y, from_x[i + 1] if recv else x]
        else:
            ref = tiles.at[from_y[i + 1] if recv else y]
        getattr(remote(ref, X if n == 0 else Y, i, tile_sems, (n, i)), what)()

    for i in three:
        go_t("start", 0, i)

    for load in loads:
        load.wait()

    def term(half, a, j):
        dims = (X, Y) if half == 0 else (Y, X)
        there = shifted(shifted(me, dims[0], a), dims[1], j)
        begin = pl.multiple_of((there[0] * 4 + there[1]) * 1024 + half * 512, 512)
        block = trail[:, :, pl.ds(begin, 512)].reshape(128, 512)
        return multiply(lhs, stacked(block))

    def send(src, dst, dim, dist, slot):
        copy = pltpu.make_async_remote_copy(
            src_ref=src, dst_ref=dst, send_sem=r_send.at[slot], recv_sem=r_recv.at[slot],
            device_id=peer(dim, dist), device_id_type=MESH,
        )
        copy.start()
        return copy

    DIM = ((X, Y), (Y, X))
    top, low = pl.ds(0, 32), pl.ds(32, 32)
    one, two, third, fourth = {}, {}, {}, {}
    for n, j in enumerate(ORDER):
        for h in range(2):
            first_out[h, n] = term(h, 2, j)
            slot = (h * 4 + n) * 2
            one[h, n, 0] = send(first_out.at[h, n, top], first_in.at[h, n, 0], DIM[h][0], 1, slot)
            one[h, n, 1] = send(first_out.at[h, n, low], first_in.at[h, n, 1], DIM[h][0], 3, slot + 1)
        if n == 0:
            for i in three:
                go_t("wait_recv", 0, i)
            for i in three:
                go_t("start", 1, i)
    def pass_on(n):
        for h in range(2):
            slot = 16 + (h * 4 + n) * 2
            for s, a in enumerate((1, 3)):
                second_out[h, n, s] = term(h, a, ORDER[n])
                one[h, n, s].wait_recv()
                rows = top if s == 0 else low
                second_out[h, n, s, rows] += first_in[h, n, s]
                two[h, n, s] = send(second_out.at[h, n, s], second_in.at[h, n, s], DIM[h][0], a, slot + s)

    def finish(n):
        j = ORDER[n]
        for h in range(2):
            third_out[h, n] = term(h, 0, j)
        for h in range(2):
            for s in range(2):
                two[h, n, s].wait_recv()
            third_out[h, n] += second_in[h, n, 0] + second_in[h, n, 1]
            if j == 2:
                third[h, 0] = send(third_out.at[h, n, top], third_in.at[h, 0], DIM[h][1], 1, 32 + h * 4)
                third[h, 1] = send(third_out.at[h, n, low], third_in.at[h, 1], DIM[h][1], 3, 33 + h * 4)
            elif j == 0:
                for s in range(2):
                    fourth[h, s].wait_recv()
                total = third_out[h, n] + fourth_in[h, 0] + fourth_in[h, 1]
                cols = pl.ds(h * 512, 512)
                updated_ref[:, :, cols] = trail_rhs[:, :, cols] - total.reshape(2, 32, 512)
            else:
                s = 0 if j == 1 else 1
                rows = top if s == 0 else low
                third[h, s].wait_recv()
                third_out[h, n, rows] += third_in[h, s]
                fourth[h, s] = send(third_out.at[h, n], fourth_in.at[h, s], DIM[h][1], j, 34 + h * 4 + s)

    pass_on(0)
    pass_on(1)
    finish(0)
    pass_on(2)
    finish(1)
    pass_on(3)
    finish(2)
    finish(3)

    for i in three:
        go_t("wait_recv", 1, i)
    parts = tiles[...].reshape(16, 8, 128)
    places = lax.broadcasted_iota(jnp.int32, (1, 128), 1)
    sums = jnp.zeros((1, 128), F32)
    for n in range(4):
        patch = ((row * 8 + col) * 4 + n).astype(F32)
        chosen = jnp.where(parts[:, 1, :] == patch, parts[:, 0, :], 0.0)
        sums = jnp.where(places == n, jnp.sum(chosen, keepdims=True), sums)
    gradient_ref[...] = sums[:, :4]

    for i in three:
        go_y("wait_send", i)
        go_r("wait_send", i)
        for n in range(4):
            go_chain("wait_send", i, n)
        go_z("wait_send", i)
        for n in range(2):
            go_t("wait_send", n, i)
    for py in range(4):
        for i in three:
            go_x("wait_send", py, i)
        for px in range(4):
            go_k("wait_send", py, px)
    for group in (one, two, third, fourth):
        for copy in group.values():
            copy.wait_send()


def on_device(upper_block, block_inverse, panel_rhs, upper_trail, trail_rhs, currents, owner):
    vmem = pl.BlockSpec(memory_space=pltpu.VMEM)
    hbm = pl.BlockSpec(memory_space=pltpu.HBM)
    dma = pltpu.SemaphoreType.DMA
    solved, updated, gradient = pl.pallas_call(
        body,
        out_shape=(
            pltpu.VMEM((2, 32, 64), F32),
            pltpu.VMEM((2, 32, 1024), F32),
            pltpu.VMEM((1, 4), F32),
        ),
        in_specs=[hbm] * 7,
        out_specs=(vmem, vmem, vmem),
        scratch_shapes=[
            pltpu.VMEM((2, 64, 128), F32),
            pltpu.VMEM((2, 64, 64), F32),
            pltpu.VMEM((2, 32, 64), F32),
            pltpu.VMEM((2, 64), F32),
            pltpu.VMEM((1, 64), jnp.int32),
            pltpu.VMEM((4, 4, 2, 128, 128), F32),
            pltpu.VMEM((4, 32, 128), F32),
            pltpu.VMEM((64, 256), F32),
            pltpu.VMEM((4, 4, 32, 128), F32),
            pltpu.VMEM((4, 4, 256, 256), BF16),
            pltpu.VMEM((2, 64, 16384), F32),
            pltpu.VMEM((2, 32, 1024), F32),
            pltpu.VMEM((2, 4, 64, 512), F32),
            pltpu.VMEM((2, 4, 2, 32, 512), F32),
            pltpu.VMEM((2, 4, 2, 64, 512), F32),
            pltpu.VMEM((2, 4, 2, 64, 512), F32),
            pltpu.VMEM((2, 4, 64, 512), F32),
            pltpu.VMEM((2, 2, 32, 512), F32),
            pltpu.VMEM((2, 2, 64, 512), F32),
            pltpu.VMEM((4, 4, 8, 128), F32),
            dma((10,)),
            dma((40,)), dma((40,)),
            *(
                dma(shape)
                for shape in (
                    (3,), (4, 3), (3,), (3,), (4, 4), (3, 4), (2, 3)
                )
                for _ in range(2)
            ),
        ],
        compiler_params=pltpu.CompilerParams(
            collective_id=0, has_side_effects=True, vmem_limit_bytes=63 * 2**20
        ),
        name="panel",
    )(upper_block, block_inverse, panel_rhs, upper_trail, trail_rhs, currents, owner.reshape(1, 64))
    return solved, updated, gradient.reshape(4)


def solution(mesh):
    return jax.shard_map(
        on_device,
        mesh=mesh,
        in_specs=(
            P(None, "row", "col"),
            P(None, "row", None),
            P(None, None, "row"),
            P(None, "row", "col"),
            P(None, None, ("col", "row")),
            P(None, "row"),
            P("row"),
        ),
        out_specs=(P(None, None, "row"), P(None, None, ("col", "row")), P(("row", "col"))),
        check_vma=False,
    )
```

```python
import jax
import jax.numpy as jnp
from jax import lax
from jax.experimental import pallas as pl
from jax.experimental.pallas import tpu as pltpu
from jax.sharding import PartitionSpec as P

MESH = pl.DeviceIdType.MESH
F32 = jnp.float32
BF16 = jnp.bfloat16
Y, X, Z = 0, 1, 2
DISTS = (1, 3, 2)
ORDER = (2, 1, 3, 0)
CUT, LAG = 1, 2
UNITS = tuple((j, c) for j in ORDER for c in range(CUT))
WIDE = 512 // CUT


def halves(value):
    high = value.astype(BF16)
    low = (value - high.astype(F32)).astype(BF16)
    return high, low


def stacked(value):
    high, low = halves(value)
    return jnp.concatenate([high, low], axis=0)


def left_side(value):
    high, low = halves(value)
    both = jnp.concatenate([high, low], axis=0)
    return jnp.concatenate([both, both], axis=1)


def multiply(left, right):
    out = jnp.dot(left, right, preferred_element_type=F32)
    rows = out.shape[0] // 2
    return out[:rows] + out[rows:]


def conj_left(value):
    re, im = value[:, :64], value[:, 64:]
    turned = jnp.concatenate([im, -re], axis=1)
    return left_side(jnp.concatenate([value, turned], axis=0))


def body(
    upper_hbm, inverse_hbm, rhs_hbm, trail_hbm, trail_rhs_hbm, currents_hbm, owner_hbm,
    solved_ref, updated_ref, gradient_ref,
    upper_ref, inverse_ref, rhs_ref, currents_ref, owner_ref, pieces, rhs_all, held, answers, weights, trail, trail_rhs,
    first_out, first_in, second_out, second_in, third_out, third_in, fourth_in, tiles,
    local_sem, r_send, r_recv, *pairs,
):
    (y_sems, x_sems, z_sems, rhs_sems, k_sems, chain_sems, tile_sems) = zip(
        pairs[::2], pairs[1::2]
    )
    row, col = lax.axis_index("row"), lax.axis_index("col")
    me = (row // 4, row % 4, col // 2)
    core = col % 2

    def shifted(coords, dim, dist):
        moved = list(coords)
        moved[dim] = (moved[dim] + dist) % 4
        return tuple(moved)

    def device(coords, which):
        return (coords[0] * 4 + coords[1], coords[2] * 2 + which)

    def peer(dim, dist):
        if dim is None:
            return device(me, 1 - core)
        return device(shifted(me, dim, dist), core)

    early = []
    for n, (src, dst) in enumerate((
        (upper_hbm, upper_ref), (inverse_hbm, inverse_ref), (rhs_hbm, rhs_ref), (currents_hbm, currents_ref), (owner_hbm, owner_ref)
    )):
        early.append(pltpu.make_async_copy(src, dst, local_sem.at[5 + n]))
        early[n].start()
    loads = []
    for part in range(4):
        cols = pl.ds(part * 4096, 4096)
        loads.append(pltpu.make_async_copy(trail_hbm.at[:, :, cols], trail.at[:, :, cols], local_sem.at[part]))
    loads.append(pltpu.make_async_copy(trail_rhs_hbm, trail_rhs, local_sem.at[4]))
    for load in loads:
        load.start()

    barrier = pltpu.get_barrier_semaphore()
    for dim in (Y, X, Z):
        for dist in DISTS:
            pl.semaphore_signal(barrier, inc=1, device_id=peer(dim, dist), device_id_type=MESH)
    pl.semaphore_signal(barrier, inc=1, device_id=peer(None, 0), device_id_type=MESH)
    for dist in DISTS:
        there = shifted(shifted(me, Y, dist), Z, dist)
        pl.semaphore_signal(barrier, inc=1, device_id=device(there, core), device_id_type=MESH)

    for load in early:
        load.wait()

    upper = upper_ref[...].reshape(128, 128)
    inv_re, inv_im = inverse_ref[0], inverse_ref[1]
    left = jnp.concatenate(
        [jnp.concatenate([inv_re, -inv_im], axis=1), jnp.concatenate([inv_im, inv_re], axis=1)], axis=0
    )
    pieces[me[0], me[1], core] = multiply(left_side(left), stacked(upper))
    rhs_all[me[1]] = jnp.concatenate([rhs_ref[0], rhs_ref[1]], axis=1)

    pl.semaphore_wait(barrier, 13)

    y, x, z = me

    def turn(at, dist):
        moved = at + dist
        return jnp.where(moved >= 4, moved - 4, moved)

    FULL = (0,) + DISTS
    from_y = [turn(y, (4 - d) % 4) for d in FULL]
    from_x = [turn(x, (4 - d) % 4) for d in FULL]
    to_y = [turn(y, d) for d in FULL]
    to_x = [turn(x, d) for d in FULL]
    to_z = [turn(z, d) for d in FULL]
    peers = {
        Y: [(v * 4 + x, col) for v in to_y],
        X: [(y * 4 + v, col) for v in to_x],
        Z: [(row, v * 2 + core) for v in to_z],
        None: [(row, col + 1 - 2 * core)] * 4,
        "YZ": [(v * 4 + x, w * 2 + core) for v, w in zip(to_y, to_z)],
    }
    solver = y == z
    three = range(3)

    def both(first, second):
        return jnp.logical_and(first, second)

    def remote(ref, dim, i, sems, index, there=None):
        return pltpu.make_async_remote_copy(
            src_ref=ref, dst_ref=ref, send_sem=sems[0].at[index], recv_sem=sems[1].at[index if there is None else there],
            device_id=peers[dim][i + 1], device_id_type=MESH,
        )

    def run(what, cond, ref, dim, i, sems, index, there=None):
        pl.when(cond)(lambda: getattr(remote(ref(), dim, i, sems, index, there), what)())

    def needed(py, px, which):
        return jnp.logical_or(py < y, both(py == y, (px + 1) // 2 <= which))

    def go_y(what, i):
        if what == "wait_recv":
            py, cond = from_y[i + 1], both(solver, from_y[i + 1] < y)
        else:
            py, cond = y, both(y < z, to_y[i + 1] == z)
        run(what, cond, lambda: pieces.at[py, x, core], Y, i, y_sems, i)

    def go_x(what, py, i):
        px = from_x[i + 1] if what == "wait_recv" else x
        run(what, both(both(solver, py <= y), needed(py, px, core)), lambda: pieces.at[py, px, core], X, i, x_sems, (py, i))

    def go_r(what, i):
        px = from_x[i + 1] if what == "wait_recv" else x
        run(what, solver, lambda: rhs_all.at[px], X, i, rhs_sems, i)

    def go_k(what, py, px):
        which = 1 - core if what == "wait_recv" else core
        run(what, both(both(solver, py <= y), needed(py, px, which)), lambda: pieces.at[py, px, which], None, 0, k_sems, (py, px))

    def go_chain(what, i, n):
        if what == "wait_recv":
            at, cond = from_y[i + 1], both(solver, from_y[i + 1] < y)
        else:
            at, cond = y, both(solver, y < to_y[i + 1])
        run(what, cond, lambda: answers.at[at, n], "YZ", i, chain_sems, (i, n))

    def go_z(what, i):
        cond = turn(z, 4 - DISTS[i]) == y if what == "wait_recv" else solver
        run(what, cond, lambda: answers.at[y, x], Z, i, z_sems, i)

    for i in three:
        go_y("start", i)
    for i in three:
        go_x("start", y, i)
    go_k("start", y, x)
    for i in three:
        go_r("start", i)
    for i in three:
        go_y("wait_recv", i)
        for j in three:
            pl.when(from_y[i + 1] < y)(lambda i=i, j=j: go_x("start", from_y[i + 1], j))
        pl.when(from_y[i + 1] < y)(lambda i=i: go_k("start", from_y[i + 1], x))

    def upto(count, action):
        def step(index, carry):
            action(index)
            return carry
        lax.fori_loop(0, count, step, 0)

    lanes = lax.broadcasted_iota(jnp.int32, (32, 128), 1)

    @pl.when(solver)
    def _():
        def collect(py):
            for i in three:
                go_x("wait_recv", py, i)
                go_k("start", py, from_x[i + 1])

        upto(y + 1, collect)
        for i in three:
            go_r("wait_recv", i)

        def split(py):
            for px in range(4):
                go_k("wait_recv", py, px)
            for px in range(4):
                for which in range(2):
                    weights[py, px, :, which * 128:(which + 1) * 128] = stacked(pieces[py, px, which])

        upto(y + 1, split)
        held[...] = jnp.zeros_like(held)

        def earlier(at):
            for px in range(4):
                for i in three:
                    pl.when(from_y[i + 1] == at)(lambda i=i: go_chain("wait_recv", i, px))
                held[...] += multiply(conj_left(answers[at, px]), weights[at, px])

        upto(y, earlier)
        for n in range(4):
            tile = held[:, (n // 2) * 128:(n // 2 + 1) * 128]
            if n % 2 == 0:
                local = jnp.where(lanes < 64, tile[:32], pltpu.roll(tile[32:], 64, 1))
            else:
                local = jnp.where(lanes < 64, pltpu.roll(tile[:32], 64, 1), tile[32:])
            answer = rhs_all[n] - local
            answers[y, n] = answer
            for i in three:
                pl.when(y < to_y[i + 1])(lambda i=i: go_chain("start", i, n))

            @pl.when(x == n)
            def _():
                for i in three:
                    go_z("start", i)

            first = (n + 1) // 2 * 128
            if first < 256:
                held[:, first:] += multiply(conj_left(answer), weights[y, n, :, first:])

    for i in three:
        go_z("wait_recv", i)

    value = multiply(conj_left(answers[y, x]), stacked(inverse_ref[...].reshape(128, 64)))
    solved_ref[...] = value.reshape(2, 32, 64)
    lhs = conj_left(jnp.concatenate([value[:32], value[32:]], axis=1))

    total_re = jnp.sum(value[:32], axis=0, keepdims=True)
    total_im = jnp.sum(value[32:], axis=0, keepdims=True)
    partial_value = currents_ref[0:1, :] * total_re - currents_ref[1:2, :] * total_im
    tiles[me[0], me[1], 0:1, 0:64] = partial_value
    tiles[me[0], me[1], 1:2, 0:64] = owner_ref[...].astype(F32)
    tiles[me[0], me[1], 0:2, 64:128] = jnp.full((2, 64), -1.0, F32)
    tiles[me[0], me[1], 2:8, :] = jnp.zeros((6, 128), F32)
    def go_t(what, n, i):
        recv = what == "wait_recv"
        if n == 0:
            ref = tiles.at[y, from_x[i + 1] if recv else x]
        else:
            ref = tiles.at[from_y[i + 1] if recv else y]
        getattr(remote(ref, X if n == 0 else Y, i, tile_sems, (n, i)), what)()

    for i in three:
        go_t("start", 0, i)

    for load in loads:
        load.wait()

    def term(half, a, unit):
        j, c = UNITS[unit]
        dims = (X, Y) if half == 0 else (Y, X)
        there = shifted(shifted(me, dims[0], a), dims[1], j)
        begin = pl.multiple_of((there[0] * 4 + there[1]) * 1024 + (half * 512 + c * WIDE), WIDE)
        block = trail[:, :, pl.ds(begin, WIDE)].reshape(128, WIDE)
        return multiply(lhs, stacked(block))

    def send(src, dst, dim, dist, slot):
        copy = pltpu.make_async_remote_copy(
            src_ref=src, dst_ref=dst, send_sem=r_send.at[slot], recv_sem=r_recv.at[slot],
            device_id=peer(dim, dist), device_id_type=MESH,
        )
        copy.start()
        return copy

    DIM = ((X, Y), (Y, X))
    top, low = pl.ds(0, 32), pl.ds(32, 32)
    one, two, third, fourth = {}, {}, {}, {}
    count = len(UNITS)
    for n in range(count):
        for h in range(2):
            first_out[h, n] = term(h, 2, n)
            slot = (h * count + n) * 2
            one[h, n, 0] = send(first_out.at[h, n, top], first_in.at[h, n, 0], DIM[h][0], 1, slot)
            one[h, n, 1] = send(first_out.at[h, n, low], first_in.at[h, n, 1], DIM[h][0], 3, slot + 1)

    def pass_on(n):
        for h in range(2):
            slot = (2 * count + h * count + n) * 2
            for s, a in enumerate((1, 3)):
                second_out[h, n, s] = term(h, a, n)
                one[h, n, s].wait_recv()
                rows = top if s == 0 else low
                second_out[h, n, s, rows] += first_in[h, n, s]
                two[h, n, s] = send(second_out.at[h, n, s], second_in.at[h, n, s], DIM[h][0], a, slot + s)

    def finish(n):
        j, c = UNITS[n]
        for h in range(2):
            third_out[h, n] = term(h, 0, n)
        for h in range(2):
            slot = 8 * count + (h * CUT + c) * 4
            for s in range(2):
                two[h, n, s].wait_recv()
            third_out[h, n] += second_in[h, n, 0] + second_in[h, n, 1]
            if j == 2:
                third[h, c, 0] = send(third_out.at[h, n, top], third_in.at[h, c, 0], DIM[h][1], 1, slot)
                third[h, c, 1] = send(third_out.at[h, n, low], third_in.at[h, c, 1], DIM[h][1], 3, slot + 1)
            elif j == 0:
                for s in range(2):
                    fourth[h, c, s].wait_recv()
                total = third_out[h, n] + fourth_in[h, c, 0] + fourth_in[h, c, 1]
                cols = pl.ds(h * 512 + c * WIDE, WIDE)
                updated_ref[:, :, cols] = trail_rhs[:, :, cols] - total.reshape(2, 32, WIDE)
            else:
                s = 0 if j == 1 else 1
                rows = top if s == 0 else low
                third[h, c, s].wait_recv()
                third_out[h, n, rows] += third_in[h, c, s]
                fourth[h, c, s] = send(third_out.at[h, n], fourth_in.at[h, c, s], DIM[h][1], j, slot + 2 + s)

    for n in range(count + LAG):
        if n >= LAG:
            finish(n - LAG)
        if n < count:
            pass_on(n)
        if n == LAG:
            for i in three:
                go_t("wait_recv", 0, i)
            for i in three:
                go_t("start", 1, i)

    for i in three:
        go_t("wait_recv", 1, i)
    parts = tiles[...].reshape(16, 8, 128)
    places = lax.broadcasted_iota(jnp.int32, (1, 128), 1)
    sums = jnp.zeros((1, 128), F32)
    for n in range(4):
        patch = ((row * 8 + col) * 4 + n).astype(F32)
        chosen = jnp.where(parts[:, 1, :] == patch, parts[:, 0, :], 0.0)
        sums = jnp.where(places == n, jnp.sum(chosen, keepdims=True), sums)
    gradient_ref[...] = sums[:, :4]

    for i in three:
        go_y("wait_send", i)
        go_r("wait_send", i)
        for n in range(4):
            go_chain("wait_send", i, n)
        go_z("wait_send", i)
        for n in range(2):
            go_t("wait_send", n, i)
    for py in range(4):
        for i in three:
            go_x("wait_send", py, i)
        for px in range(4):
            go_k("wait_send", py, px)
    for group in (one, two, third, fourth):
        for copy in group.values():
            copy.wait_send()


def on_device(upper_block, block_inverse, panel_rhs, upper_trail, trail_rhs, currents, owner):
    vmem = pl.BlockSpec(memory_space=pltpu.VMEM)
    hbm = pl.BlockSpec(memory_space=pltpu.HBM)
    dma = pltpu.SemaphoreType.DMA
    solved, updated, gradient = pl.pallas_call(
        body,
        out_shape=(
            pltpu.VMEM((2, 32, 64), F32),
            pltpu.VMEM((2, 32, 1024), F32),
            pltpu.VMEM((1, 4), F32),
        ),
        in_specs=[hbm] * 7,
        out_specs=(vmem, vmem, vmem),
        scratch_shapes=[
            pltpu.VMEM((2, 64, 128), F32),
            pltpu.VMEM((2, 64, 64), F32),
            pltpu.VMEM((2, 32, 64), F32),
            pltpu.VMEM((2, 64), F32),
            pltpu.VMEM((1, 64), jnp.int32),
            pltpu.VMEM((4, 4, 2, 128, 128), F32),
            pltpu.VMEM((4, 32, 128), F32),
            pltpu.VMEM((64, 256), F32),
            pltpu.VMEM((4, 4, 32, 128), F32),
            pltpu.VMEM((4, 4, 256, 256), BF16),
            pltpu.VMEM((2, 64, 16384), F32),
            pltpu.VMEM((2, 32, 1024), F32),
            pltpu.VMEM((2, 4 * CUT, 64, WIDE), F32),
            pltpu.VMEM((2, 4 * CUT, 2, 32, WIDE), F32),
            pltpu.VMEM((2, 4 * CUT, 2, 64, WIDE), F32),
            pltpu.VMEM((2, 4 * CUT, 2, 64, WIDE), F32),
            pltpu.VMEM((2, 4 * CUT, 64, WIDE), F32),
            pltpu.VMEM((2, CUT, 2, 32, WIDE), F32),
            pltpu.VMEM((2, CUT, 2, 64, WIDE), F32),
            pltpu.VMEM((4, 4, 8, 128), F32),
            dma((10,)),
            dma((40 * CUT,)), dma((40 * CUT,)),
            *(
                dma(shape)
                for shape in (
                    (3,), (4, 3), (3,), (3,), (4, 4), (3, 4), (2, 3)
                )
                for _ in range(2)
            ),
        ],
        compiler_params=pltpu.CompilerParams(
            collective_id=0, has_side_effects=True, vmem_limit_bytes=63 * 2**20
        ),
        name="panel",
    )(upper_block, block_inverse, panel_rhs, upper_trail, trail_rhs, currents, owner.reshape(1, 64))
    return solved, updated, gradient.reshape(4)


def solution(mesh):
    return jax.shard_map(
        on_device,
        mesh=mesh,
        in_specs=(
            P(None, "row", "col"),
            P(None, "row", None),
            P(None, None, "row"),
            P(None, "row", "col"),
            P(None, None, ("col", "row")),
            P(None, "row"),
            P("row"),
        ),
        out_specs=(P(None, None, "row"), P(None, None, ("col", "row")), P(("row", "col"))),
        check_vma=False,
    )
```

```python
import jax
import jax.numpy as jnp
from jax import lax
from jax.experimental import pallas as pl
from jax.experimental.pallas import tpu as pltpu
from jax.sharding import PartitionSpec as P

MESH = pl.DeviceIdType.MESH
F32 = jnp.float32
BF16 = jnp.bfloat16
Y, X, Z = 0, 1, 2
DISTS = (1, 3, 2)
ORDER = (2, 1, 3, 0)
CUT = 1
STEPS = ("p0", "p1", "f0", "p2", "tiles", "p3", "f1", "f2", "patches", "f3")
UNITS = tuple((j, c) for j in ORDER for c in range(CUT))
WIDE = 512 // CUT


def halves(value):
    high = value.astype(BF16)
    low = (value - high.astype(F32)).astype(BF16)
    return high, low


def stacked(value):
    high, low = halves(value)
    return jnp.concatenate([high, low], axis=0)


def left_side(value):
    high, low = halves(value)
    both = jnp.concatenate([high, low], axis=0)
    return jnp.concatenate([both, both], axis=1)


def multiply(left, right):
    out = jnp.dot(left, right, preferred_element_type=F32)
    rows = out.shape[0] // 2
    return out[:rows] + out[rows:]


def conj_left(value):
    re, im = value[:, :64], value[:, 64:]
    turned = jnp.concatenate([im, -re], axis=1)
    return left_side(jnp.concatenate([value, turned], axis=0))


def body(
    upper_hbm, inverse_hbm, rhs_hbm, trail_hbm, trail_rhs_hbm, currents_hbm, owner_hbm,
    solved_ref, updated_ref, gradient_ref,
    upper_ref, inverse_ref, rhs_ref, currents_ref, owner_ref, pieces, rhs_all, held, answers, weights, inverse_w, trail, trail_rhs,
    first_out, first_in, second_out, second_in, third_out, third_in, fourth_in, tiles,
    local_sem, r_send, r_recv, *pairs,
):
    (y_sems, x_sems, z_sems, rhs_sems, k_sems, chain_sems, tile_sems) = zip(
        pairs[::2], pairs[1::2]
    )
    row, col = lax.axis_index("row"), lax.axis_index("col")
    me = (row // 4, row % 4, col // 2)
    core = col % 2

    def shifted(coords, dim, dist):
        moved = list(coords)
        moved[dim] = (moved[dim] + dist) % 4
        return tuple(moved)

    def device(coords, which):
        return (coords[0] * 4 + coords[1], coords[2] * 2 + which)

    def peer(dim, dist):
        if dim is None:
            return device(me, 1 - core)
        return device(shifted(me, dim, dist), core)

    early = []
    for n, (src, dst) in enumerate((
        (upper_hbm, upper_ref), (inverse_hbm, inverse_ref), (rhs_hbm, rhs_ref), (currents_hbm, currents_ref), (owner_hbm, owner_ref)
    )):
        early.append(pltpu.make_async_copy(src, dst, local_sem.at[5 + n]))
        early[n].start()
    loads = []
    for part in range(4):
        cols = pl.ds(part * 4096, 4096)
        loads.append(pltpu.make_async_copy(trail_hbm.at[:, :, cols], trail.at[:, :, cols], local_sem.at[part]))
    loads.append(pltpu.make_async_copy(trail_rhs_hbm, trail_rhs, local_sem.at[4]))
    for load in loads:
        load.start()

    barrier = pltpu.get_barrier_semaphore()
    for dim in (Y, X, Z):
        for dist in DISTS:
            pl.semaphore_signal(barrier, inc=1, device_id=peer(dim, dist), device_id_type=MESH)
    pl.semaphore_signal(barrier, inc=1, device_id=peer(None, 0), device_id_type=MESH)
    for dist in DISTS:
        there = shifted(shifted(me, Y, dist), Z, dist)
        pl.semaphore_signal(barrier, inc=1, device_id=device(there, core), device_id_type=MESH)

    for load in early:
        load.wait()

    upper = upper_ref[...].reshape(128, 128)
    inv_re, inv_im = inverse_ref[0], inverse_ref[1]
    left = jnp.concatenate(
        [jnp.concatenate([inv_re, -inv_im], axis=1), jnp.concatenate([inv_im, inv_re], axis=1)], axis=0
    )
    pieces[me[0], me[1], core] = multiply(left_side(left), stacked(upper))
    rhs_all[me[1]] = jnp.concatenate([rhs_ref[0], rhs_ref[1]], axis=1)

    pl.semaphore_wait(barrier, 13)

    y, x, z = me

    def turn(at, dist):
        moved = at + dist
        return jnp.where(moved >= 4, moved - 4, moved)

    FULL = (0,) + DISTS
    from_y = [turn(y, (4 - d) % 4) for d in FULL]
    from_x = [turn(x, (4 - d) % 4) for d in FULL]
    to_y = [turn(y, d) for d in FULL]
    to_x = [turn(x, d) for d in FULL]
    to_z = [turn(z, d) for d in FULL]
    peers = {
        Y: [(v * 4 + x, col) for v in to_y],
        X: [(y * 4 + v, col) for v in to_x],
        Z: [(row, v * 2 + core) for v in to_z],
        None: [(row, col + 1 - 2 * core)] * 4,
        "YZ": [(v * 4 + x, w * 2 + core) for v, w in zip(to_y, to_z)],
    }
    solver = y == z
    three = range(3)

    def both(first, second):
        return jnp.logical_and(first, second)

    def remote(ref, dim, i, sems, index, there=None):
        return pltpu.make_async_remote_copy(
            src_ref=ref, dst_ref=ref, send_sem=sems[0].at[index], recv_sem=sems[1].at[index if there is None else there],
            device_id=peers[dim][i + 1], device_id_type=MESH,
        )

    def run(what, cond, ref, dim, i, sems, index, there=None):
        pl.when(cond)(lambda: getattr(remote(ref(), dim, i, sems, index, there), what)())

    def needed(py, px, which):
        return jnp.logical_or(py < y, both(py == y, (px + 1) // 2 <= which))

    def go_y(what, i):
        if what == "wait_recv":
            py, cond = from_y[i + 1], both(solver, from_y[i + 1] < y)
        else:
            py, cond = y, both(y < z, to_y[i + 1] == z)
        run(what, cond, lambda: pieces.at[py, x, core], Y, i, y_sems, i)

    def go_x(what, py, i):
        px = from_x[i + 1] if what == "wait_recv" else x
        run(what, both(both(solver, py <= y), needed(py, px, core)), lambda: pieces.at[py, px, core], X, i, x_sems, (py, i))

    def go_r(what, i):
        px = from_x[i + 1] if what == "wait_recv" else x
        run(what, solver, lambda: rhs_all.at[px], X, i, rhs_sems, i)

    def go_k(what, py, px):
        which = 1 - core if what == "wait_recv" else core
        run(what, both(both(solver, py <= y), needed(py, px, which)), lambda: pieces.at[py, px, which], None, 0, k_sems, (py, px))

    def go_chain(what, i, n):
        if what == "wait_recv":
            at, cond = from_y[i + 1], both(solver, from_y[i + 1] < y)
        else:
            at, cond = y, both(solver, y < to_y[i + 1])
        run(what, cond, lambda: answers.at[at, n], "YZ", i, chain_sems, (i, n))

    def go_z(what, i):
        cond = turn(z, 4 - DISTS[i]) == y if what == "wait_recv" else solver
        run(what, cond, lambda: answers.at[y, x], Z, i, z_sems, i)

    for i in three:
        go_y("start", i)
    for i in three:
        go_x("start", y, i)
    go_k("start", y, x)
    for i in three:
        go_r("start", i)
    for i in three:
        go_y("wait_recv", i)
        for j in three:
            pl.when(from_y[i + 1] < y)(lambda i=i, j=j: go_x("start", from_y[i + 1], j))
        pl.when(from_y[i + 1] < y)(lambda i=i: go_k("start", from_y[i + 1], x))

    def upto(count, action):
        def step(index, carry):
            action(index)
            return carry
        lax.fori_loop(0, count, step, 0)

    lanes = lax.broadcasted_iota(jnp.int32, (32, 128), 1)

    @pl.when(solver)
    def _():
        def collect(py):
            for i in three:
                go_x("wait_recv", py, i)
                go_k("start", py, from_x[i + 1])

        upto(y + 1, collect)
        for i in three:
            go_r("wait_recv", i)

        def split(py):
            for px in range(4):
                go_k("wait_recv", py, px)
            for px in range(4):
                for which in range(2):
                    weights[py, px, :, which * 128:(which + 1) * 128] = stacked(pieces[py, px, which])

        upto(y + 1, split)
        held[...] = jnp.zeros_like(held)

        def earlier(at):
            for px in range(4):
                for i in three:
                    pl.when(from_y[i + 1] == at)(lambda i=i: go_chain("wait_recv", i, px))
                held[...] += multiply(conj_left(answers[at, px]), weights[at, px])

        upto(y, earlier)
        for n in range(4):
            tile = held[:, (n // 2) * 128:(n // 2 + 1) * 128]
            if n % 2 == 0:
                local = jnp.where(lanes < 64, tile[:32], pltpu.roll(tile[32:], 64, 1))
            else:
                local = jnp.where(lanes < 64, pltpu.roll(tile[:32], 64, 1), tile[32:])
            answer = rhs_all[n] - local
            answers[y, n] = answer
            for i in three:
                pl.when(y < to_y[i + 1])(lambda i=i: go_chain("start", i, n))

            @pl.when(x == n)
            def _():
                for i in three:
                    go_z("start", i)

            first = (n + 1) // 2 * 128
            if first < 256:
                held[:, first:] += multiply(conj_left(answer), weights[y, n, :, first:])

    for load in loads:
        load.wait()
    inverse_w[...] = stacked(inverse_ref[...].reshape(128, 64))
    for i in three:
        go_z("wait_recv", i)

    value = multiply(conj_left(answers[y, x]), inverse_w[...])
    lhs = conj_left(jnp.concatenate([value[:32], value[32:]], axis=1))

    def partials():
        solved_ref[...] = value.reshape(2, 32, 64)
        total_re = jnp.sum(value[:32], axis=0, keepdims=True)
        total_im = jnp.sum(value[32:], axis=0, keepdims=True)
        partial_value = currents_ref[0:1, :] * total_re - currents_ref[1:2, :] * total_im
        tiles[me[0], me[1], 0:1, 0:64] = partial_value
        tiles[me[0], me[1], 1:2, 0:64] = owner_ref[...].astype(F32)
        tiles[me[0], me[1], 0:2, 64:128] = jnp.full((2, 64), -1.0, F32)
        tiles[me[0], me[1], 2:8, :] = jnp.zeros((6, 128), F32)
        for i in three:
            go_t("start", 0, i)

    def go_t(what, n, i):
        recv = what == "wait_recv"
        if n == 0:
            ref = tiles.at[y, from_x[i + 1] if recv else x]
        else:
            ref = tiles.at[from_y[i + 1] if recv else y]
        getattr(remote(ref, X if n == 0 else Y, i, tile_sems, (n, i)), what)()

    def term(half, a, unit):
        j, c = UNITS[unit]
        dims = (X, Y) if half == 0 else (Y, X)
        there = shifted(shifted(me, dims[0], a), dims[1], j)
        begin = pl.multiple_of((there[0] * 4 + there[1]) * 1024 + (half * 512 + c * WIDE), WIDE)
        block = trail[:, :, pl.ds(begin, WIDE)].reshape(128, WIDE)
        return multiply(lhs, stacked(block))

    def send(src, dst, dim, dist, slot):
        copy = pltpu.make_async_remote_copy(
            src_ref=src, dst_ref=dst, send_sem=r_send.at[slot], recv_sem=r_recv.at[slot],
            device_id=peer(dim, dist), device_id_type=MESH,
        )
        copy.start()
        return copy

    DIM = ((X, Y), (Y, X))
    top, low = pl.ds(0, 32), pl.ds(32, 32)
    one, two, third, fourth = {}, {}, {}, {}
    count = len(UNITS)
    for n in range(count):
        for h in range(2):
            first_out[h, n] = term(h, 2, n)
            slot = (h * count + n) * 2
            one[h, n, 0] = send(first_out.at[h, n, top], first_in.at[h, n, 0], DIM[h][0], 1, slot)
            one[h, n, 1] = send(first_out.at[h, n, low], first_in.at[h, n, 1], DIM[h][0], 3, slot + 1)
        if n == 1:
            partials()

    def pass_on(n):
        for h in range(2):
            slot = (2 * count + h * count + n) * 2
            for s, a in enumerate((1, 3)):
                second_out[h, n, s] = term(h, a, n)
                one[h, n, s].wait_recv()
                rows = top if s == 0 else low
                second_out[h, n, s, rows] += first_in[h, n, s]
                two[h, n, s] = send(second_out.at[h, n, s], second_in.at[h, n, s], DIM[h][0], a, slot + s)

    def finish(n):
        j, c = UNITS[n]
        for h in range(2):
            third_out[h, n] = term(h, 0, n)
        for h in range(2):
            slot = 8 * count + (h * CUT + c) * 4
            for s in range(2):
                two[h, n, s].wait_recv()
            third_out[h, n] += second_in[h, n, 0] + second_in[h, n, 1]
            if j == 2:
                third[h, c, 0] = send(third_out.at[h, n, top], third_in.at[h, c, 0], DIM[h][1], 1, slot)
                third[h, c, 1] = send(third_out.at[h, n, low], third_in.at[h, c, 1], DIM[h][1], 3, slot + 1)
            elif j == 0:
                for s in range(2):
                    fourth[h, c, s].wait_recv()
                total = third_out[h, n] + fourth_in[h, c, 0] + fourth_in[h, c, 1]
                cols = pl.ds(h * 512 + c * WIDE, WIDE)
                updated_ref[:, :, cols] = trail_rhs[:, :, cols] - total.reshape(2, 32, WIDE)
            else:
                s = 0 if j == 1 else 1
                rows = top if s == 0 else low
                third[h, c, s].wait_recv()
                third_out[h, n, rows] += third_in[h, c, s]
                fourth[h, c, s] = send(third_out.at[h, n], fourth_in.at[h, c, s], DIM[h][1], j, slot + 2 + s)

    def gather_patches():
        for i in three:
            go_t("wait_recv", 1, i)
        parts = tiles[...].reshape(16, 8, 128)
        places = lax.broadcasted_iota(jnp.int32, (1, 128), 1)
        sums = jnp.zeros((1, 128), F32)
        for n in range(4):
            patch = ((row * 8 + col) * 4 + n).astype(F32)
            chosen = jnp.where(parts[:, 1, :] == patch, parts[:, 0, :], 0.0)
            sums = jnp.where(places == n, jnp.sum(chosen, keepdims=True), sums)
        gradient_ref[...] = sums[:, :4]

        for i in three:
            go_y("wait_send", i)
            go_r("wait_send", i)
            for n in range(4):
                go_chain("wait_send", i, n)
            go_z("wait_send", i)
            for n in range(2):
                go_t("wait_send", n, i)
        for py in range(4):
            for i in three:
                go_x("wait_send", py, i)
            for px in range(4):
                go_k("wait_send", py, px)

    for step in STEPS:
        if step == "tiles":
            for i in three:
                go_t("wait_recv", 0, i)
            for i in three:
                go_t("start", 1, i)
        elif step == "patches":
            gather_patches()
        elif step[0] == "p":
            pass_on(int(step[1]))
        else:
            finish(int(step[1]))

    for group in (one, two, third, fourth):
        for copy in group.values():
            copy.wait_send()


def on_device(upper_block, block_inverse, panel_rhs, upper_trail, trail_rhs, currents, owner):
    vmem = pl.BlockSpec(memory_space=pltpu.VMEM)
    hbm = pl.BlockSpec(memory_space=pltpu.HBM)
    dma = pltpu.SemaphoreType.DMA
    solved, updated, gradient = pl.pallas_call(
        body,
        out_shape=(
            pltpu.VMEM((2, 32, 64), F32),
            pltpu.VMEM((2, 32, 1024), F32),
            pltpu.VMEM((1, 4), F32),
        ),
        in_specs=[hbm] * 7,
        out_specs=(vmem, vmem, vmem),
        scratch_shapes=[
            pltpu.VMEM((2, 64, 128), F32),
            pltpu.VMEM((2, 64, 64), F32),
            pltpu.VMEM((2, 32, 64), F32),
            pltpu.VMEM((2, 64), F32),
            pltpu.VMEM((1, 64), jnp.int32),
            pltpu.VMEM((4, 4, 2, 128, 128), F32),
            pltpu.VMEM((4, 32, 128), F32),
            pltpu.VMEM((64, 256), F32),
            pltpu.VMEM((4, 4, 32, 128), F32),
            pltpu.VMEM((4, 4, 256, 256), BF16),
            pltpu.VMEM((256, 64), BF16),
            pltpu.VMEM((2, 64, 16384), F32),
            pltpu.VMEM((2, 32, 1024), F32),
            pltpu.VMEM((2, 4 * CUT, 64, WIDE), F32),
            pltpu.VMEM((2, 4 * CUT, 2, 32, WIDE), F32),
            pltpu.VMEM((2, 4 * CUT, 2, 64, WIDE), F32),
            pltpu.VMEM((2, 4 * CUT, 2, 64, WIDE), F32),
            pltpu.VMEM((2, 4 * CUT, 64, WIDE), F32),
            pltpu.VMEM((2, CUT, 2, 32, WIDE), F32),
            pltpu.VMEM((2, CUT, 2, 64, WIDE), F32),
            pltpu.VMEM((4, 4, 8, 128), F32),
            dma((10,)),
            dma((40 * CUT,)), dma((40 * CUT,)),
            *(
                dma(shape)
                for shape in (
                    (3,), (4, 3), (3,), (3,), (4, 4), (3, 4), (2, 3)
                )
                for _ in range(2)
            ),
        ],
        compiler_params=pltpu.CompilerParams(
            collective_id=0, has_side_effects=True, vmem_limit_bytes=63 * 2**20
        ),
        name="panel",
    )(upper_block, block_inverse, panel_rhs, upper_trail, trail_rhs, currents, owner.reshape(1, 64))
    return solved, updated, gradient.reshape(4)


def solution(mesh):
    return jax.shard_map(
        on_device,
        mesh=mesh,
        in_specs=(
            P(None, "row", "col"),
            P(None, "row", None),
            P(None, None, "row"),
            P(None, "row", "col"),
            P(None, None, ("col", "row")),
            P(None, "row"),
            P("row"),
        ),
        out_specs=(P(None, None, "row"), P(None, None, ("col", "row")), P(("row", "col"))),
        check_vma=False,
    )
```

```python
import jax
import jax.numpy as jnp
from jax import lax
from jax.experimental import pallas as pl
from jax.experimental.pallas import tpu as pltpu
from jax.sharding import PartitionSpec as P

MESH = pl.DeviceIdType.MESH
F32 = jnp.float32
BF16 = jnp.bfloat16
Y, X, Z = 0, 1, 2
DISTS = (1, 3, 2)
ORDER = (2, 1, 3, 0)
CUT = 1
STEPS = ("p0", "p1", "f0", "p2", "tiles", "p3", "f1", "f2", "patches", "f3")
UNITS = tuple((j, c) for j in ORDER for c in range(CUT))
WIDE = 512 // CUT


def halves(value):
    high = value.astype(BF16)
    low = (value - high.astype(F32)).astype(BF16)
    return high, low


def stacked(value):
    high, low = halves(value)
    return jnp.concatenate([high, low], axis=0)


def left_side(value):
    high, low = halves(value)
    both = jnp.concatenate([high, low], axis=0)
    return jnp.concatenate([both, both], axis=1)


def multiply(left, right):
    out = jnp.dot(left, right, preferred_element_type=F32)
    rows = out.shape[0] // 2
    return out[:rows] + out[rows:]


def conj_left(value):
    re, im = value[:, :64], value[:, 64:]
    turned = jnp.concatenate([im, -re], axis=1)
    return left_side(jnp.concatenate([value, turned], axis=0))


def body(
    upper_hbm, inverse_hbm, rhs_hbm, trail_hbm, trail_rhs_hbm, currents_hbm, owner_hbm,
    solved_ref, updated_ref, gradient_ref,
    upper_ref, inverse_ref, rhs_ref, currents_ref, owner_ref, pieces, rhs_all, held, answers, answer_halves, weights, inverse_w, trail, trail_rhs,
    first_out, first_in, second_out, second_in, third_out, third_in, fourth_in, tiles,
    local_sem, r_send, r_recv, *pairs,
):
    (y_sems, x_sems, z_sems, rhs_sems, k_sems, chain_sems, tile_sems) = zip(
        pairs[::2], pairs[1::2]
    )
    row, col = lax.axis_index("row"), lax.axis_index("col")
    me = (row // 4, row % 4, col // 2)
    core = col % 2

    def shifted(coords, dim, dist):
        moved = list(coords)
        moved[dim] = (moved[dim] + dist) % 4
        return tuple(moved)

    def device(coords, which):
        return (coords[0] * 4 + coords[1], coords[2] * 2 + which)

    def peer(dim, dist):
        if dim is None:
            return device(me, 1 - core)
        return device(shifted(me, dim, dist), core)

    early = []
    for n, (src, dst) in enumerate((
        (upper_hbm, upper_ref), (inverse_hbm, inverse_ref), (rhs_hbm, rhs_ref), (currents_hbm, currents_ref), (owner_hbm, owner_ref)
    )):
        early.append(pltpu.make_async_copy(src, dst, local_sem.at[5 + n]))
        early[n].start()
    loads = []
    for part in range(4):
        cols = pl.ds(part * 4096, 4096)
        loads.append(pltpu.make_async_copy(trail_hbm.at[:, :, cols], trail.at[:, :, cols], local_sem.at[part]))
    loads.append(pltpu.make_async_copy(trail_rhs_hbm, trail_rhs, local_sem.at[4]))
    for load in loads:
        load.start()

    barrier = pltpu.get_barrier_semaphore()
    for dim in (Y, X, Z):
        for dist in DISTS:
            pl.semaphore_signal(barrier, inc=1, device_id=peer(dim, dist), device_id_type=MESH)
    pl.semaphore_signal(barrier, inc=1, device_id=peer(None, 0), device_id_type=MESH)
    for dist in DISTS:
        there = shifted(shifted(me, Y, dist), Z, dist)
        pl.semaphore_signal(barrier, inc=1, device_id=device(there, core), device_id_type=MESH)
        pl.semaphore_signal(barrier, inc=1, device_id=device(shifted(me, Z, dist), 1 - core), device_id_type=MESH)

    for load in early:
        load.wait()

    upper = upper_ref[...].reshape(128, 128)
    inv_re, inv_im = inverse_ref[0], inverse_ref[1]
    left = jnp.concatenate(
        [jnp.concatenate([inv_re, -inv_im], axis=1), jnp.concatenate([inv_im, inv_re], axis=1)], axis=0
    )
    pieces[me[0], me[1], core] = multiply(left_side(left), stacked(upper))
    mine = pl.ds(pl.multiple_of(core * 16, 16), 16)
    rhs_all[me[1]] = jnp.concatenate([rhs_ref[0, mine], rhs_ref[1, mine]], axis=1)

    pl.semaphore_wait(barrier, 16)

    y, x, z = me

    def turn(at, dist):
        moved = at + dist
        return jnp.where(moved >= 4, moved - 4, moved)

    FULL = (0,) + DISTS
    from_y = [turn(y, (4 - d) % 4) for d in FULL]
    from_x = [turn(x, (4 - d) % 4) for d in FULL]
    to_y = [turn(y, d) for d in FULL]
    to_x = [turn(x, d) for d in FULL]
    to_z = [turn(z, d) for d in FULL]
    peers = {
        Y: [(v * 4 + x, col) for v in to_y],
        X: [(y * 4 + v, col) for v in to_x],
        Z: [(row, v * 2 + core) for v in to_z],
        None: [(row, col + 1 - 2 * core)] * 4,
        "YZ": [(v * 4 + x, w * 2 + core) for v, w in zip(to_y, to_z)],
    }
    solver = y == z
    three = range(3)

    def both(first, second):
        return jnp.logical_and(first, second)

    def remote(ref, dim, i, sems, index, there=None):
        return pltpu.make_async_remote_copy(
            src_ref=ref, dst_ref=ref, send_sem=sems[0].at[index], recv_sem=sems[1].at[index if there is None else there],
            device_id=dim if isinstance(dim, tuple) else peers[dim][i + 1], device_id_type=MESH,
        )

    def run(what, cond, ref, dim, i, sems, index, there=None):
        pl.when(cond)(lambda: getattr(remote(ref(), dim, i, sems, index, there), what)())

    def needed(py, px, which):
        return jnp.logical_or(py < y, both(py == y, (px + 1) // 2 <= which))

    def go_y(what, i):
        if what == "wait_recv":
            py, cond = from_y[i + 1], both(solver, from_y[i + 1] < y)
        else:
            py, cond = y, both(y < z, to_y[i + 1] == z)
        run(what, cond, lambda: pieces.at[py, x, core], Y, i, y_sems, i)

    def go_x(what, py, i):
        px = from_x[i + 1] if what == "wait_recv" else x
        run(what, both(both(solver, py <= y), needed(py, px, core)), lambda: pieces.at[py, px, core], X, i, x_sems, (py, i))

    def go_r(what, i):
        px = from_x[i + 1] if what == "wait_recv" else x
        run(what, solver, lambda: rhs_all.at[px], X, i, rhs_sems, i)

    def go_k(what, py, px):
        which = 1 - core if what == "wait_recv" else core
        run(what, both(both(solver, py <= y), needed(py, px, which)), lambda: pieces.at[py, px, which], None, 0, k_sems, (py, px))

    def go_chain(what, i, n):
        if what == "wait_recv":
            at, cond = from_y[i + 1], both(solver, from_y[i + 1] < y)
        else:
            at, cond = y, both(solver, y < to_y[i + 1])
        run(what, cond, lambda: answers.at[at, n], "YZ", i, chain_sems, (i, n))

    def go_z(what, i, cross):
        recv = what == "wait_recv"
        k = (1 - core if cross else core) if recv else core
        if i == 3:
            cond, there = y == z, (row, col + 1 - 2 * core)
        else:
            cond = turn(z, 4 - DISTS[i]) == y if recv else y == z
            there = (row, to_z[i + 1] * 2 + (1 - core if cross else core))
        run(what, cond, lambda: answer_halves.at[k], there, i, z_sems, (i, cross))

    targets = [(i, cross) for i in three for cross in (0, 1)] + [(3, 1)]

    for i in three:
        go_y("start", i)
    for i in three:
        go_x("start", y, i)
    go_k("start", y, x)
    for i in three:
        go_r("start", i)
    for i in three:
        go_y("wait_recv", i)
        for j in three:
            pl.when(from_y[i + 1] < y)(lambda i=i, j=j: go_x("start", from_y[i + 1], j))
        pl.when(from_y[i + 1] < y)(lambda i=i: go_k("start", from_y[i + 1], x))

    def upto(count, action):
        def step(index, carry):
            action(index)
            return carry
        lax.fori_loop(0, count, step, 0)

    lanes = lax.broadcasted_iota(jnp.int32, (16, 128), 1)

    @pl.when(solver)
    def _():
        def collect(py):
            for i in three:
                go_x("wait_recv", py, i)
                go_k("start", py, from_x[i + 1])

        upto(y + 1, collect)
        for i in three:
            go_r("wait_recv", i)

        def split(py):
            for px in range(4):
                go_k("wait_recv", py, px)
            for px in range(4):
                for which in range(2):
                    weights[py, px, :, which * 128:(which + 1) * 128] = stacked(pieces[py, px, which])

        upto(y + 1, split)
        held[...] = jnp.zeros_like(held)

        def earlier(at):
            for px in range(4):
                for i in three:
                    pl.when(from_y[i + 1] == at)(lambda i=i: go_chain("wait_recv", i, px))
                held[...] += multiply(conj_left(answers[at, px]), weights[at, px])

        upto(y, earlier)
        for n in range(4):
            tile = held[:, (n // 2) * 128:(n // 2 + 1) * 128]
            if n % 2 == 0:
                local = jnp.where(lanes < 64, tile[:16], pltpu.roll(tile[16:], 64, 1))
            else:
                local = jnp.where(lanes < 64, pltpu.roll(tile[:16], 64, 1), tile[16:])
            answer = rhs_all[n] - local
            answers[y, n] = answer
            for i in three:
                pl.when(y < to_y[i + 1])(lambda i=i: go_chain("start", i, n))

            @pl.when(x == n)
            def _():
                answer_halves[core] = answer
                for i, cross in targets:
                    go_z("start", i, cross)

            first = (n + 1) // 2 * 128
            if first < 256:
                held[:, first:] += multiply(conj_left(answer), weights[y, n, :, first:])

    for load in loads:
        load.wait()
    inverse_w[...] = stacked(inverse_ref[...].reshape(128, 64))
    for i, cross in targets:
        go_z("wait_recv", i, cross)

    value = multiply(conj_left(answer_halves[...].reshape(32, 128)), inverse_w[...])
    lhs = conj_left(jnp.concatenate([value[:32], value[32:]], axis=1))

    def partials():
        solved_ref[...] = value.reshape(2, 32, 64)
        total_re = jnp.sum(value[:32], axis=0, keepdims=True)
        total_im = jnp.sum(value[32:], axis=0, keepdims=True)
        partial_value = currents_ref[0:1, :] * total_re - currents_ref[1:2, :] * total_im
        tiles[me[0], me[1], 0:1, 0:64] = partial_value
        tiles[me[0], me[1], 1:2, 0:64] = owner_ref[...].astype(F32)
        tiles[me[0], me[1], 0:2, 64:128] = jnp.full((2, 64), -1.0, F32)
        tiles[me[0], me[1], 2:8, :] = jnp.zeros((6, 128), F32)
        for i in three:
            go_t("start", 0, i)

    def go_t(what, n, i):
        recv = what == "wait_recv"
        if n == 0:
            ref = tiles.at[y, from_x[i + 1] if recv else x]
        else:
            ref = tiles.at[from_y[i + 1] if recv else y]
        getattr(remote(ref, X if n == 0 else Y, i, tile_sems, (n, i)), what)()

    def term(half, a, unit):
        j, c = UNITS[unit]
        dims = (X, Y) if half == 0 else (Y, X)
        there = shifted(shifted(me, dims[0], a), dims[1], j)
        begin = pl.multiple_of((there[0] * 4 + there[1]) * 1024 + (half * 512 + c * WIDE), WIDE)
        block = trail[:, :, pl.ds(begin, WIDE)].reshape(128, WIDE)
        return multiply(lhs, stacked(block))

    def send(src, dst, dim, dist, slot):
        copy = pltpu.make_async_remote_copy(
            src_ref=src, dst_ref=dst, send_sem=r_send.at[slot], recv_sem=r_recv.at[slot],
            device_id=peer(dim, dist), device_id_type=MESH,
        )
        copy.start()
        return copy

    DIM = ((X, Y), (Y, X))
    top, low = pl.ds(0, 32), pl.ds(32, 32)
    one, two, third, fourth = {}, {}, {}, {}
    count = len(UNITS)
    for n in range(count):
        for h in range(2):
            first_out[h, n] = term(h, 2, n)
            slot = (h * count + n) * 2
            one[h, n, 0] = send(first_out.at[h, n, top], first_in.at[h, n, 0], DIM[h][0], 1, slot)
            one[h, n, 1] = send(first_out.at[h, n, low], first_in.at[h, n, 1], DIM[h][0], 3, slot + 1)
        if n == 1:
            partials()

    def pass_on(n):
        for h in range(2):
            slot = (2 * count + h * count + n) * 2
            for s, a in enumerate((1, 3)):
                second_out[h, n, s] = term(h, a, n)
                one[h, n, s].wait_recv()
                rows = top if s == 0 else low
                second_out[h, n, s, rows] += first_in[h, n, s]
                two[h, n, s] = send(second_out.at[h, n, s], second_in.at[h, n, s], DIM[h][0], a, slot + s)

    def finish(n):
        j, c = UNITS[n]
        for h in range(2):
            third_out[h, n] = term(h, 0, n)
        for h in range(2):
            slot = 8 * count + (h * CUT + c) * 4
            for s in range(2):
                two[h, n, s].wait_recv()
            third_out[h, n] += second_in[h, n, 0] + second_in[h, n, 1]
            if j == 2:
                third[h, c, 0] = send(third_out.at[h, n, top], third_in.at[h, c, 0], DIM[h][1], 1, slot)
                third[h, c, 1] = send(third_out.at[h, n, low], third_in.at[h, c, 1], DIM[h][1], 3, slot + 1)
            elif j == 0:
                for s in range(2):
                    fourth[h, c, s].wait_recv()
                total = third_out[h, n] + fourth_in[h, c, 0] + fourth_in[h, c, 1]
                cols = pl.ds(h * 512 + c * WIDE, WIDE)
                updated_ref[:, :, cols] = trail_rhs[:, :, cols] - total.reshape(2, 32, WIDE)
            else:
                s = 0 if j == 1 else 1
                rows = top if s == 0 else low
                third[h, c, s].wait_recv()
                third_out[h, n, rows] += third_in[h, c, s]
                fourth[h, c, s] = send(third_out.at[h, n], fourth_in.at[h, c, s], DIM[h][1], j, slot + 2 + s)

    def gather_patches():
        for i in three:
            go_t("wait_recv", 1, i)
        parts = tiles[...].reshape(16, 8, 128)
        places = lax.broadcasted_iota(jnp.int32, (1, 128), 1)
        sums = jnp.zeros((1, 128), F32)
        for n in range(4):
            patch = ((row * 8 + col) * 4 + n).astype(F32)
            chosen = jnp.where(parts[:, 1, :] == patch, parts[:, 0, :], 0.0)
            sums = jnp.where(places == n, jnp.sum(chosen, keepdims=True), sums)
        gradient_ref[...] = sums[:, :4]

        for i in three:
            go_y("wait_send", i)
            go_r("wait_send", i)
            for n in range(4):
                go_chain("wait_send", i, n)
            for cross in (0, 1):
                go_z("wait_send", i, cross)
            for n in range(2):
                go_t("wait_send", n, i)
        for py in range(4):
            for i in three:
                go_x("wait_send", py, i)
            for px in range(4):
                go_k("wait_send", py, px)
        go_z("wait_send", 3, 1)

    for step in STEPS:
        if step == "tiles":
            for i in three:
                go_t("wait_recv", 0, i)
            for i in three:
                go_t("start", 1, i)
        elif step == "patches":
            gather_patches()
        elif step[0] == "p":
            pass_on(int(step[1]))
        else:
            finish(int(step[1]))

    for group in (one, two, third, fourth):
        for copy in group.values():
            copy.wait_send()


def on_device(upper_block, block_inverse, panel_rhs, upper_trail, trail_rhs, currents, owner):
    vmem = pl.BlockSpec(memory_space=pltpu.VMEM)
    hbm = pl.BlockSpec(memory_space=pltpu.HBM)
    dma = pltpu.SemaphoreType.DMA
    solved, updated, gradient = pl.pallas_call(
        body,
        out_shape=(
            pltpu.VMEM((2, 32, 64), F32),
            pltpu.VMEM((2, 32, 1024), F32),
            pltpu.VMEM((1, 4), F32),
        ),
        in_specs=[hbm] * 7,
        out_specs=(vmem, vmem, vmem),
        scratch_shapes=[
            pltpu.VMEM((2, 64, 128), F32),
            pltpu.VMEM((2, 64, 64), F32),
            pltpu.VMEM((2, 32, 64), F32),
            pltpu.VMEM((2, 64), F32),
            pltpu.VMEM((1, 64), jnp.int32),
            pltpu.VMEM((4, 4, 2, 128, 128), F32),
            pltpu.VMEM((4, 16, 128), F32),
            pltpu.VMEM((32, 256), F32),
            pltpu.VMEM((4, 4, 16, 128), F32),
            pltpu.VMEM((2, 16, 128), F32),
            pltpu.VMEM((4, 4, 256, 256), BF16),
            pltpu.VMEM((256, 64), BF16),
            pltpu.VMEM((2, 64, 16384), F32),
            pltpu.VMEM((2, 32, 1024), F32),
            pltpu.VMEM((2, 4 * CUT, 64, WIDE), F32),
            pltpu.VMEM((2, 4 * CUT, 2, 32, WIDE), F32),
            pltpu.VMEM((2, 4 * CUT, 2, 64, WIDE), F32),
            pltpu.VMEM((2, 4 * CUT, 2, 64, WIDE), F32),
            pltpu.VMEM((2, 4 * CUT, 64, WIDE), F32),
            pltpu.VMEM((2, CUT, 2, 32, WIDE), F32),
            pltpu.VMEM((2, CUT, 2, 64, WIDE), F32),
            pltpu.VMEM((4, 4, 8, 128), F32),
            dma((10,)),
            dma((40 * CUT,)), dma((40 * CUT,)),
            *(
                dma(shape)
                for shape in (
                    (3,), (4, 3), (4, 2), (3,), (4, 4), (3, 4), (2, 3)
                )
                for _ in range(2)
            ),
        ],
        compiler_params=pltpu.CompilerParams(
            collective_id=0, has_side_effects=True, vmem_limit_bytes=63 * 2**20
        ),
        name="panel",
    )(upper_block, block_inverse, panel_rhs, upper_trail, trail_rhs, currents, owner.reshape(1, 64))
    return solved, updated, gradient.reshape(4)


def solution(mesh):
    return jax.shard_map(
        on_device,
        mesh=mesh,
        in_specs=(
            P(None, "row", "col"),
            P(None, "row", None),
            P(None, None, "row"),
            P(None, "row", "col"),
            P(None, None, ("col", "row")),
            P(None, "row"),
            P("row"),
        ),
        out_specs=(P(None, None, "row"), P(None, None, ("col", "row")), P(("row", "col"))),
        check_vma=False,
    )
```

```python
import jax
import jax.numpy as jnp
from jax import lax
from jax.experimental import pallas as pl
from jax.experimental.pallas import tpu as pltpu
from jax.sharding import PartitionSpec as P

MESH = pl.DeviceIdType.MESH
F32 = jnp.float32
BF16 = jnp.bfloat16
Y, X, Z = 0, 1, 2
DISTS = (1, 3, 2)
ORDER = (2, 1, 3, 0)
CUT = 1
STEPS = ("p0", "p1", "f0", "p2", "tiles", "p3", "f1", "f2", "patches", "f3")
UNITS = tuple((j, c) for j in ORDER for c in range(CUT))
WIDE = 512 // CUT


def halves(value):
    high = value.astype(BF16)
    low = (value - high.astype(F32)).astype(BF16)
    return high, low


def stacked(value):
    high, low = halves(value)
    return jnp.concatenate([high, low], axis=0)


def left_side(value):
    high, low = halves(value)
    both = jnp.concatenate([high, low], axis=0)
    return jnp.concatenate([both, both], axis=1)


def multiply(left, right):
    out = jnp.dot(left, right, preferred_element_type=F32)
    rows = out.shape[0] // 2
    return out[:rows] + out[rows:]


def conj_left(value):
    re, im = value[:, :64], value[:, 64:]
    turned = jnp.concatenate([im, -re], axis=1)
    return left_side(jnp.concatenate([value, turned], axis=0))


def body(
    upper_hbm, inverse_hbm, rhs_hbm, trail_hbm, trail_rhs_hbm, currents_hbm, owner_hbm,
    solved_ref, updated_ref, gradient_ref,
    upper_ref, inverse_ref, rhs_ref, currents_ref, owner_ref, pieces, rhs_all, held, answers, answer_halves, weights, inverse_w, trail, trail_rhs,
    first_out, first_in, second_out, second_in, third_out, third_in, fourth_in, tiles,
    local_sem, r_send, r_recv, *pairs,
):
    (y_sems, x_sems, z_sems, rhs_sems, k_sems, chain_sems, tile_sems) = zip(
        pairs[::2], pairs[1::2]
    )
    row, col = lax.axis_index("row"), lax.axis_index("col")
    me = (row // 4, row % 4, col // 2)
    core = col % 2

    def shifted(coords, dim, dist):
        moved = list(coords)
        moved[dim] = (moved[dim] + dist) % 4
        return tuple(moved)

    def device(coords, which):
        return (coords[0] * 4 + coords[1], coords[2] * 2 + which)

    def peer(dim, dist):
        if dim is None:
            return device(me, 1 - core)
        return device(shifted(me, dim, dist), core)

    early = []
    for n, (src, dst) in enumerate((
        (upper_hbm, upper_ref), (inverse_hbm, inverse_ref), (rhs_hbm, rhs_ref), (currents_hbm, currents_ref), (owner_hbm, owner_ref)
    )):
        early.append(pltpu.make_async_copy(src, dst, local_sem.at[5 + n]))
        early[n].start()
    loads = []
    for part in range(4):
        cols = pl.ds(part * 4096, 4096)
        loads.append(pltpu.make_async_copy(trail_hbm.at[:, :, cols], trail.at[:, :, cols], local_sem.at[part]))
    loads.append(pltpu.make_async_copy(trail_rhs_hbm, trail_rhs, local_sem.at[4]))
    for load in loads:
        load.start()

    barrier = pltpu.get_barrier_semaphore()
    for dim in (Y, X, Z):
        for dist in DISTS:
            pl.semaphore_signal(barrier, inc=1, device_id=peer(dim, dist), device_id_type=MESH)
    pl.semaphore_signal(barrier, inc=1, device_id=peer(None, 0), device_id_type=MESH)
    for dist in DISTS:
        there = shifted(shifted(me, Y, dist), Z, dist)
        pl.semaphore_signal(barrier, inc=1, device_id=device(there, core), device_id_type=MESH)
        pl.semaphore_signal(barrier, inc=1, device_id=device(shifted(me, Z, dist), 1 - core), device_id_type=MESH)

    for load in early:
        load.wait()

    upper = upper_ref[...].reshape(128, 128)
    inv_re, inv_im = inverse_ref[0], inverse_ref[1]
    left = jnp.concatenate(
        [jnp.concatenate([inv_re, -inv_im], axis=1), jnp.concatenate([inv_im, inv_re], axis=1)], axis=0
    )
    pieces[me[0], me[1], core] = multiply(left_side(left), stacked(upper))
    mine = pl.ds(pl.multiple_of(core * 16, 16), 16)
    rhs_all[me[1]] = jnp.concatenate([rhs_ref[0, mine], rhs_ref[1, mine]], axis=1)

    pl.semaphore_wait(barrier, 16)

    y, x, z = me

    def turn(at, dist):
        moved = at + dist
        return jnp.where(moved >= 4, moved - 4, moved)

    FULL = (0,) + DISTS
    from_y = [turn(y, (4 - d) % 4) for d in FULL]
    from_x = [turn(x, (4 - d) % 4) for d in FULL]
    to_y = [turn(y, d) for d in FULL]
    to_x = [turn(x, d) for d in FULL]
    to_z = [turn(z, d) for d in FULL]
    peers = {
        Y: [(v * 4 + x, col) for v in to_y],
        X: [(y * 4 + v, col) for v in to_x],
        Z: [(row, v * 2 + core) for v in to_z],
        None: [(row, col + 1 - 2 * core)] * 4,
        "YZ": [(v * 4 + x, w * 2 + core) for v, w in zip(to_y, to_z)],
    }
    solver = y == z
    three = range(3)

    def both(first, second):
        return jnp.logical_and(first, second)

    def remote(ref, dim, i, sems, index, there=None):
        return pltpu.make_async_remote_copy(
            src_ref=ref, dst_ref=ref, send_sem=sems[0].at[index], recv_sem=sems[1].at[index if there is None else there],
            device_id=dim if isinstance(dim, tuple) else peers[dim][i + 1], device_id_type=MESH,
        )

    def run(what, cond, ref, dim, i, sems, index, there=None):
        pl.when(cond)(lambda: getattr(remote(ref(), dim, i, sems, index, there), what)())

    def needed(py, px, which):
        return jnp.logical_or(py < y, both(py == y, (px + 1) // 2 <= which))

    def go_y(what, i):
        if what == "wait_recv":
            py, cond = from_y[i + 1], both(solver, from_y[i + 1] < y)
        else:
            py, cond = y, both(y < z, to_y[i + 1] == z)
        run(what, cond, lambda: pieces.at[py, x, core], Y, i, y_sems, i)

    def go_x(what, py, i):
        px = from_x[i + 1] if what == "wait_recv" else x
        run(what, both(both(solver, py <= y), needed(py, px, core)), lambda: pieces.at[py, px, core], X, i, x_sems, (py, i))

    def go_r(what, i):
        px = from_x[i + 1] if what == "wait_recv" else x
        run(what, solver, lambda: rhs_all.at[px], X, i, rhs_sems, i)

    def go_k(what, py, px):
        which = 1 - core if what == "wait_recv" else core
        run(what, both(both(solver, py <= y), needed(py, px, which)), lambda: pieces.at[py, px, which], None, 0, k_sems, (py, px))

    def go_chain(what, i, n):
        if what == "wait_recv":
            at, cond = from_y[i + 1], both(solver, from_y[i + 1] < y)
        else:
            at, cond = y, both(solver, y < to_y[i + 1])
        run(what, cond, lambda: answers.at[at, n], "YZ", i, chain_sems, (i, n))

    def go_z(what, i, cross):
        recv = what == "wait_recv"
        k = (1 - core if cross else core) if recv else core
        if i == 3:
            cond, there = y == z, (row, col + 1 - 2 * core)
        else:
            cond = turn(z, 4 - DISTS[i]) == y if recv else y == z
            there = (row, to_z[i + 1] * 2 + (1 - core if cross else core))
        run(what, cond, lambda: answer_halves.at[k], there, i, z_sems, (i, cross))

    targets = [(i, cross) for i in three for cross in (0, 1)] + [(3, 1)]

    for i in three:
        go_y("start", i)
    for i in three:
        go_x("start", y, i)
    go_k("start", y, x)
    for i in three:
        go_r("start", i)
    for i in three:
        go_y("wait_recv", i)
        for j in three:
            pl.when(from_y[i + 1] < y)(lambda i=i, j=j: go_x("start", from_y[i + 1], j))
        pl.when(from_y[i + 1] < y)(lambda i=i: go_k("start", from_y[i + 1], x))

    def upto(count, action):
        def step(index, carry):
            action(index)
            return carry
        lax.fori_loop(0, count, step, 0)

    lanes = lax.broadcasted_iota(jnp.int32, (16, 128), 1)

    @pl.when(solver)
    def _():
        def collect(py):
            for i in three:
                go_x("wait_recv", py, i)
                go_k("start", py, from_x[i + 1])

        upto(y + 1, collect)
        for i in three:
            go_r("wait_recv", i)

        def split(py):
            for px in range(4):
                go_k("wait_recv", py, px)
            for px in range(4):
                for which in range(2):
                    weights[py, px, :, which * 128:(which + 1) * 128] = stacked(pieces[py, px, which])

        upto(y + 1, split)
        held[...] = jnp.zeros_like(held)

        def earlier(at):
            for px in range(4):
                for i in three:
                    pl.when(from_y[i + 1] == at)(lambda i=i: go_chain("wait_recv", i, px))
                held[...] += multiply(conj_left(answers[at, px]), weights[at, px])

        upto(y, earlier)
        for n in range(4):
            tile = held[:, (n // 2) * 128:(n // 2 + 1) * 128]
            if n % 2 == 0:
                local = jnp.where(lanes < 64, tile[:16], pltpu.roll(tile[16:], 64, 1))
            else:
                local = jnp.where(lanes < 64, pltpu.roll(tile[:16], 64, 1), tile[16:])
            answer = rhs_all[n] - local
            answers[y, n] = answer
            for i in three:
                pl.when(y < to_y[i + 1])(lambda i=i: go_chain("start", i, n))

            @pl.when(x == n)
            def _():
                answer_halves[core] = answer
                for i, cross in targets:
                    go_z("start", i, cross)

            first = (n + 1) // 2 * 128
            if first < 256:
                held[:, first:] += multiply(conj_left(answer), weights[y, n, :, first:])

    for load in loads:
        load.wait()
    inverse_w[...] = stacked(inverse_ref[...].reshape(128, 64))
    for i, cross in targets:
        go_z("wait_recv", i, cross)

    value = multiply(conj_left(answer_halves[...].reshape(32, 128)), inverse_w[...])
    lhs = conj_left(jnp.concatenate([value[:32], value[32:]], axis=1))

    def partials():
        solved_ref[...] = value.reshape(2, 32, 64)
        total_re = jnp.sum(value[:32], axis=0, keepdims=True)
        total_im = jnp.sum(value[32:], axis=0, keepdims=True)
        partial_value = currents_ref[0:1, :] * total_re - currents_ref[1:2, :] * total_im
        tiles[me[0], me[1], 0:1, 0:64] = partial_value
        tiles[me[0], me[1], 1:2, 0:64] = owner_ref[...].astype(F32)
        tiles[me[0], me[1], 0:2, 64:128] = jnp.full((2, 64), -1.0, F32)
        tiles[me[0], me[1], 2:8, :] = jnp.zeros((6, 128), F32)
        for i in three:
            go_t("start", 0, i)

    def go_t(what, n, i):
        recv = what == "wait_recv"
        if n == 0:
            ref = tiles.at[y, from_x[i + 1] if recv else x]
        else:
            ref = tiles.at[from_y[i + 1] if recv else y]
        getattr(remote(ref, X if n == 0 else Y, i, tile_sems, (n, i)), what)()

    def term(half, a, unit):
        j, c = UNITS[unit]
        dims = (X, Y) if half == 0 else (Y, X)
        there = shifted(shifted(me, dims[0], a), dims[1], j)
        begin = pl.multiple_of((there[0] * 4 + there[1]) * 1024 + (half * 512 + c * WIDE), WIDE)
        block = trail[:, :, pl.ds(begin, WIDE)].reshape(128, WIDE)
        return multiply(lhs, stacked(block))

    def send(src, dst, dim, dist, slot):
        copy = pltpu.make_async_remote_copy(
            src_ref=src, dst_ref=dst, send_sem=r_send.at[slot], recv_sem=r_recv.at[slot],
            device_id=peer(dim, dist), device_id_type=MESH,
        )
        copy.start()
        return copy

    DIM = ((X, Y), (Y, X))
    top, low = pl.ds(0, 32), pl.ds(32, 32)
    one, two, third, fourth = {}, {}, {}, {}
    count = len(UNITS)
    for n in range(count):
        for h in range(2):
            first_out[h, n] = term(h, 2, n)
            slot = (h * count + n) * 2
            one[h, n, 0] = send(first_out.at[h, n, top], first_in.at[h, n, 0], DIM[h][0], 1, slot)
            one[h, n, 1] = send(first_out.at[h, n, low], first_in.at[h, n, 1], DIM[h][0], 3, slot + 1)
        if n == 1:
            partials()

    def pass_on(n):
        for h in (1, 0):
            slot = (2 * count + h * count + n) * 2
            for s, a in enumerate((1, 3)):
                second_out[h, n, s] = term(h, a, n)
                one[h, n, s].wait_recv()
                rows = top if s == 0 else low
                second_out[h, n, s, rows] += first_in[h, n, s]
                two[h, n, s] = send(second_out.at[h, n, s], second_in.at[h, n, s], DIM[h][0], a, slot + s)

    def finish(n):
        j, c = UNITS[n]
        for h in range(2):
            third_out[h, n] = term(h, 0, n)
        for h in range(2):
            slot = 8 * count + (h * CUT + c) * 4
            for s in range(2):
                two[h, n, s].wait_recv()
            third_out[h, n] += second_in[h, n, 0] + second_in[h, n, 1]
            if j == 2:
                third[h, c, 0] = send(third_out.at[h, n, top], third_in.at[h, c, 0], DIM[h][1], 1, slot)
                third[h, c, 1] = send(third_out.at[h, n, low], third_in.at[h, c, 1], DIM[h][1], 3, slot + 1)
            elif j == 0:
                for s in range(2):
                    fourth[h, c, s].wait_recv()
                total = third_out[h, n] + fourth_in[h, c, 0] + fourth_in[h, c, 1]
                cols = pl.ds(h * 512 + c * WIDE, WIDE)
                updated_ref[:, :, cols] = trail_rhs[:, :, cols] - total.reshape(2, 32, WIDE)
            else:
                s = 0 if j == 1 else 1
                rows = top if s == 0 else low
                third[h, c, s].wait_recv()
                third_out[h, n, rows] += third_in[h, c, s]
                fourth[h, c, s] = send(third_out.at[h, n], fourth_in.at[h, c, s], DIM[h][1], j, slot + 2 + s)

    def gather_patches():
        for i in three:
            go_t("wait_recv", 1, i)
        parts = tiles[...].reshape(16, 8, 128)
        places = lax.broadcasted_iota(jnp.int32, (1, 128), 1)
        sums = jnp.zeros((1, 128), F32)
        for n in range(4):
            patch = ((row * 8 + col) * 4 + n).astype(F32)
            chosen = jnp.where(parts[:, 1, :] == patch, parts[:, 0, :], 0.0)
            sums = jnp.where(places == n, jnp.sum(chosen, keepdims=True), sums)
        gradient_ref[...] = sums[:, :4]

        for i in three:
            go_y("wait_send", i)
            go_r("wait_send", i)
            for n in range(4):
                go_chain("wait_send", i, n)
            for cross in (0, 1):
                go_z("wait_send", i, cross)
            for n in range(2):
                go_t("wait_send", n, i)
        for py in range(4):
            for i in three:
                go_x("wait_send", py, i)
            for px in range(4):
                go_k("wait_send", py, px)
        go_z("wait_send", 3, 1)

    for step in STEPS:
        if step == "tiles":
            for i in three:
                go_t("wait_recv", 0, i)
            for i in three:
                go_t("start", 1, i)
        elif step == "patches":
            gather_patches()
        elif step[0] == "p":
            pass_on(int(step[1]))
        else:
            finish(int(step[1]))

    for group in (one, two, third, fourth):
        for copy in group.values():
            copy.wait_send()


def on_device(upper_block, block_inverse, panel_rhs, upper_trail, trail_rhs, currents, owner):
    vmem = pl.BlockSpec(memory_space=pltpu.VMEM)
    hbm = pl.BlockSpec(memory_space=pltpu.HBM)
    dma = pltpu.SemaphoreType.DMA
    solved, updated, gradient = pl.pallas_call(
        body,
        out_shape=(
            pltpu.VMEM((2, 32, 64), F32),
            pltpu.VMEM((2, 32, 1024), F32),
            pltpu.VMEM((1, 4), F32),
        ),
        in_specs=[hbm] * 7,
        out_specs=(vmem, vmem, vmem),
        scratch_shapes=[
            pltpu.VMEM((2, 64, 128), F32),
            pltpu.VMEM((2, 64, 64), F32),
            pltpu.VMEM((2, 32, 64), F32),
            pltpu.VMEM((2, 64), F32),
            pltpu.VMEM((1, 64), jnp.int32),
            pltpu.VMEM((4, 4, 2, 128, 128), F32),
            pltpu.VMEM((4, 16, 128), F32),
            pltpu.VMEM((32, 256), F32),
            pltpu.VMEM((4, 4, 16, 128), F32),
            pltpu.VMEM((2, 16, 128), F32),
            pltpu.VMEM((4, 4, 256, 256), BF16),
            pltpu.VMEM((256, 64), BF16),
            pltpu.VMEM((2, 64, 16384), F32),
            pltpu.VMEM((2, 32, 1024), F32),
            pltpu.VMEM((2, 4 * CUT, 64, WIDE), F32),
            pltpu.VMEM((2, 4 * CUT, 2, 32, WIDE), F32),
            pltpu.VMEM((2, 4 * CUT, 2, 64, WIDE), F32),
            pltpu.VMEM((2, 4 * CUT, 2, 64, WIDE), F32),
            pltpu.VMEM((2, 4 * CUT, 64, WIDE), F32),
            pltpu.VMEM((2, CUT, 2, 32, WIDE), F32),
            pltpu.VMEM((2, CUT, 2, 64, WIDE), F32),
            pltpu.VMEM((4, 4, 8, 128), F32),
            dma((10,)),
            dma((40 * CUT,)), dma((40 * CUT,)),
            *(
                dma(shape)
                for shape in (
                    (3,), (4, 3), (4, 2), (3,), (4, 4), (3, 4), (2, 3)
                )
                for _ in range(2)
            ),
        ],
        compiler_params=pltpu.CompilerParams(
            collective_id=0, has_side_effects=True, vmem_limit_bytes=63 * 2**20
        ),
        name="panel",
    )(upper_block, block_inverse, panel_rhs, upper_trail, trail_rhs, currents, owner.reshape(1, 64))
    return solved, updated, gradient.reshape(4)


def solution(mesh):
    return jax.shard_map(
        on_device,
        mesh=mesh,
        in_specs=(
            P(None, "row", "col"),
            P(None, "row", None),
            P(None, None, "row"),
            P(None, "row", "col"),
            P(None, None, ("col", "row")),
            P(None, "row"),
            P("row"),
        ),
        out_specs=(P(None, None, "row"), P(None, None, ("col", "row")), P(("row", "col"))),
        check_vma=False,
    )
```
